32 devices in a mesh: groups: 2 (over y), seq: 4 (over z), head: 2 (over x), rep: 2 (over core).
Axes of the slice: x: 2, y: 2, z: 4, core: 2. Of those that a mesh axis runs over, the one named last changes fastest.
Arguments:
- queries: bfloat16 [32, 128, 1280], P(('groups', 'seq', 'rep'), None, 'head'), parts along dimension 0, may hold values from -5.5 to 5.5
- response_keys: bfloat16 [32, 128, 256], P(('groups', 'seq', 'rep'), None, 'head'), parts along dimension 0, may hold values from -6 to 6
- response_values: bfloat16 [32, 128, 256], P(('groups', 'seq', 'rep'), None, 'head'), parts along dimension 0, may hold values from -14 to 14
- grad_out: bfloat16 [32, 128, 1280], P(('groups', 'seq', 'rep'), None, 'head'), parts along dimension 0, may hold values from -6 to 6
- prompt_keys: bfloat16 [4096, 256], P(('groups', 'seq'), 'head'), parts along dimension 0, may hold values from -5.5 to 5.5
- prompt_values: bfloat16 [4096, 256], P(('groups', 'seq'), 'head'), parts along dimension 0, may hold values from -14 to 14
- packing: int32 [32], P('groups'), parts along dimension 0, may hold values from 0 to 15, each once
- lengths: int32 [32], P(('groups', 'seq', 'rep')), parts along dimension 0, may hold values from 1 to 128
- tree_mask: int32 [32, 2], P(('groups', 'seq', 'rep')), parts along dimension 0, may hold values from 0 to 1, as said below
Outputs:
- attended: bfloat16 [32, 128, 1280], P(('groups', 'seq', 'rep'), None, 'head'), parts along dimension 0
- grad_queries: bfloat16 [32, 128, 1280], P(('groups', 'seq', 'rep'), None, 'head'), parts along dimension 0
- grad_keys: bfloat16 [32, 128, 256], P(('groups', 'seq', 'rep'), None, 'head'), parts along dimension 0
- grad_values: bfloat16 [32, 128, 256], P(('groups', 'seq', 'rep'), None, 'head'), parts along dimension 0
- prompt_grads: float32 [2, 4096, 256], P(None, ('groups', 'seq'), 'head'), parts along dimension 1
The draws below stay inside these ranges and needn't reach their ends.
There are 2 independent parts, one for each index of `groups`. The reference program is written for one: setup_inputs(seed, part) draws one part's arguments, and reference() takes and returns one part's arrays. A program takes and returns all parts, laid end to end along the dimension named above; each array names one. Nothing has to cross between parts.
Inputs may be any that keep to these rules, and one draw needn't show every extreme that they name: `tree_mask`: row s of each aligned block of 2 rows has 1 in column s and in the columns of its ancestors along a parent chain of earlier segments of the block, 0 elsewhere.
All inputs are finite; a program needn't handle non-finite values.
Results may differ from the reference program's by a relative error of at most 0.012.
The reference program's roundings to bfloat16 on the way count: a program that leaves them out, or rounds other values in their place, can miss the bound.
Values may be sent and summed in bfloat16 or wider, within the bound.
No kernel may reach another device: no remote copies, remote signals or barrier semaphores. Data moves between devices by JAX's collectives and lax.ppermute only.
A program may use at most 64 MiB of HBM per device.

```python
import jax
import jax.numpy as jnp
from jax import lax

HEAD_DIM = 128
GROUP = 5
KV_HEADS = 2
SEG_LEN = 128
SEG_DEV = 2
PROMPT = 2048
SEGS = 16


def draw_queries(key, part):
    key = jax.random.fold_in(key, 11)
    values = jnp.clip(1.5 * jax.random.normal(key, (SEGS * SEG_LEN, KV_HEADS, GROUP, HEAD_DIM), jnp.float32), -5.5, 5.5)
    return values.reshape(SEGS, SEG_LEN, KV_HEADS * GROUP * HEAD_DIM).astype(jnp.bfloat16)


def draw_prompt_keys(key, part):
    key = jax.random.fold_in(key, 13)
    values = jnp.clip(jax.random.normal(key, (PROMPT, KV_HEADS, HEAD_DIM), jnp.float32), -5.5, 5.5)
    return values.reshape(PROMPT, KV_HEADS * HEAD_DIM).astype(jnp.bfloat16)


def draw_lengths(key, part):
    key = jax.random.fold_in(key, 17)
    drawn = jax.random.randint(key, (SEGS,), 1, SEG_LEN + 1)
    return drawn.at[0].set(SEG_LEN).astype(jnp.int32)


def draw_tree_mask(key, part):
    key = jax.random.fold_in(key, 19)
    tree_count = SEGS // SEG_DEV
    noise = jax.random.randint(key, (tree_count, SEG_DEV), 0, 1 << 20)
    columns = jnp.arange(SEG_DEV)
    mask_rows = []
    for slot_index in range(SEG_DEV):
        own = jnp.broadcast_to((columns == slot_index).astype(jnp.int32)[None, :], (tree_count, SEG_DEV))
        if slot_index > 0:
            parent = noise[:, slot_index] % (slot_index + 1) - 1
            stacked = jnp.stack(mask_rows, axis=1)
            picker = (jnp.arange(slot_index)[None, :] == parent[:, None]).astype(jnp.int32)
            inherited = jnp.sum(stacked * picker[:, :, None], axis=1)
            own = jnp.maximum(own, inherited)
        mask_rows.append(own)
    return jnp.stack(mask_rows, axis=1).reshape(SEGS, SEG_DEV).astype(jnp.int32)


def level_of(own_key, dims, pieces, smallest, top_value):
    level, own = 1.0, jax.random.fold_in(own_key, 6)
    for dim, shards_of in pieces:
        steps = jnp.exp(jax.random.uniform(jax.random.fold_in(own, dim), (shards_of,), jnp.float32, smallest / len(pieces), top_value / len(pieces)))
        level = level * jnp.repeat(steps, dims[dim] // shards_of).reshape([-1 if axis == dim else 1 for axis in range(len(dims))])
    return level


def bell_draw(own_key, shape, scale, bound, cuts=(), held_as=jnp.bfloat16):
    level = level_of(own_key, shape, cuts, -0.22, 0.18) if cuts else 1.0
    result = jax.random.normal(own_key, shape, jnp.float32) * scale * level
    return jnp.minimum(jnp.maximum(result, -bound), bound).astype(held_as)


def setup_inputs(seed: int = 0, part: int = 0) -> dict:
    key_list = jax.random.split(jax.random.key(seed), 10)
    own_keys = jax.random.split(jax.random.fold_in(key_list[9], part), 10)
    queries = draw_queries(jax.random.fold_in(jax.random.fold_in(key_list[9], part), 71), part)
    response_keys = bell_draw(own_keys[1], (SEGS, SEG_LEN, KV_HEADS * HEAD_DIM), 1.0, 6.0, ((0, 8), (2, 2)))
    response_values = bell_draw(own_keys[2], (SEGS, SEG_LEN, KV_HEADS * HEAD_DIM), 2.5, 14.0, ((0, 8), (2, 2)))
    grad_out = bell_draw(own_keys[3], (SEGS, SEG_LEN, KV_HEADS * GROUP * HEAD_DIM), 1.0, 6.0, ((0, 8), (2, 2)))
    prompt_keys = draw_prompt_keys(jax.random.fold_in(jax.random.fold_in(key_list[9], part), 71), part)
    prompt_values = bell_draw(own_keys[5], (PROMPT, KV_HEADS * HEAD_DIM), 2.5, 14.0, ((0, 4), (1, 2)))
    packing = jax.random.permutation(own_keys[6], SEGS).astype(jnp.int32)
    lengths = draw_lengths(jax.random.fold_in(jax.random.fold_in(key_list[9], part), 71), part)
    tree_mask = draw_tree_mask(jax.random.fold_in(jax.random.fold_in(key_list[9], part), 71), part)
    return {"queries": queries, "response_keys": response_keys, "response_values": response_values, "grad_out": grad_out, "prompt_keys": prompt_keys, "prompt_values": prompt_values, "packing": packing, "lengths": lengths, "tree_mask": tree_mask}


def reference(queries, response_keys, response_values, grad_out, prompt_keys, prompt_values, packing, lengths, tree_mask):
    softmax_scale = HEAD_DIM ** -0.5
    tree_count = SEGS // SEG_DEV
    row_count = SEG_DEV * SEG_LEN
    head_cols = GROUP * HEAD_DIM

    def relay(source):
        return jnp.take(source, packing, axis=0).reshape(tree_count, row_count, source.shape[2])

    query_all = relay(queries)
    key_all = relay(response_keys)
    value_all = relay(response_values)
    grad_all = relay(grad_out)
    length_all = lengths.reshape(tree_count, SEG_DEV)
    tree_all = tree_mask.reshape(tree_count, SEG_DEV, SEG_DEV)
    position = jnp.arange(row_count)
    slot_of = position // SEG_LEN
    within = position % SEG_LEN

    results = []
    for head_index in range(KV_HEADS):
        head_keys = prompt_keys[:, head_index * HEAD_DIM:(head_index + 1) * HEAD_DIM].astype(jnp.float32)
        head_values = prompt_values[:, head_index * HEAD_DIM:(head_index + 1) * HEAD_DIM].astype(jnp.float32)

        def one_tree(items):
            query_rows, key_rows, value_rows, grad_rows, tree_lengths, tree_rows = items
            live_rows = within < tree_lengths[slot_of]
            live_float = live_rows.astype(jnp.float32)
            visible = (tree_rows[slot_of][:, slot_of] == 1) & live_rows[None, :]
            visible = visible & ((slot_of[:, None] != slot_of[None, :]) | (within[None, :] <= within[:, None]))
            query_heads = query_rows.reshape(row_count, GROUP, HEAD_DIM).transpose(1, 0, 2).astype(jnp.float32)
            key_float = key_rows.astype(jnp.float32)
            value_float = value_rows.astype(jnp.float32)
            prompt_scores = jnp.einsum('grd,pd->grp', query_heads, head_keys) * softmax_scale
            tree_scores = jnp.einsum('grd,sd->grs', query_heads, key_float) * softmax_scale
            tree_scores = jnp.where(visible[None], tree_scores, -1e30)
            row_max = jnp.maximum(jnp.max(prompt_scores, axis=-1), jnp.max(tree_scores, axis=-1))
            prompt_exp = jnp.exp(prompt_scores - row_max[..., None])
            tree_exp = jnp.exp(tree_scores - row_max[..., None])
            denominator = jnp.sum(prompt_exp, axis=-1) + jnp.sum(tree_exp, axis=-1)
            prompt_probs = prompt_exp / denominator[..., None]
            tree_probs = tree_exp / denominator[..., None]
            prompt_round = lax.optimization_barrier(prompt_probs.astype(jnp.bfloat16)).astype(jnp.float32)
            tree_round = lax.optimization_barrier(tree_probs.astype(jnp.bfloat16)).astype(jnp.float32)
            weighted = jnp.einsum('grp,pd->grd', prompt_round, head_values) + jnp.einsum('grs,sd->grd', tree_round, value_float)
            attended_heads = (weighted * live_float[None, :, None]).astype(jnp.bfloat16)
            grad_live = grad_rows.reshape(row_count, GROUP, HEAD_DIM).transpose(1, 0, 2).astype(jnp.float32) * live_float[None, :, None]
            delta = jnp.sum(grad_live * attended_heads.astype(jnp.float32), axis=-1)
            prompt_dprob = jnp.einsum('grd,pd->grp', grad_live, head_values)
            tree_dprob = jnp.einsum('grd,sd->grs', grad_live, value_float)
            prompt_dscore = lax.optimization_barrier((prompt_probs * (prompt_dprob - delta[..., None])).astype(jnp.bfloat16)).astype(jnp.float32)
            tree_dscore = lax.optimization_barrier((tree_probs * (tree_dprob - delta[..., None])).astype(jnp.bfloat16)).astype(jnp.float32)
            grad_query = softmax_scale * (jnp.einsum('grp,pd->grd', prompt_dscore, head_keys) + jnp.einsum('grs,sd->grd', tree_dscore, key_float))
            grad_query = grad_query.astype(jnp.bfloat16).transpose(1, 0, 2).reshape(row_count, head_cols)
            grad_key = (softmax_scale * jnp.einsum('grs,grd->sd', tree_dscore, query_heads)).astype(jnp.bfloat16)
            grad_value = jnp.einsum('grs,grd->sd', tree_round, grad_live).astype(jnp.bfloat16)
            prompt_key_grad = softmax_scale * jnp.einsum('grp,grd->pd', prompt_dscore, query_heads)
            prompt_value_grad = jnp.einsum('grp,grd->pd', prompt_round, grad_live)
            attended_rows = attended_heads.transpose(1, 0, 2).reshape(row_count, head_cols)
            return attended_rows, grad_query, grad_key, grad_value, prompt_key_grad, prompt_value_grad

        column_start = head_index * head_cols
        items = (query_all[:, :, column_start:column_start + head_cols],
                 key_all[:, :, head_index * HEAD_DIM:(head_index + 1) * HEAD_DIM],
                 value_all[:, :, head_index * HEAD_DIM:(head_index + 1) * HEAD_DIM],
                 grad_all[:, :, column_start:column_start + head_cols],
                 length_all, tree_all)
        outcome = lax.map(one_tree, items)
        results.append(outcome)

    attended = jnp.concatenate([entry[0] for entry in results], axis=-1).reshape(SEGS, SEG_LEN, KV_HEADS * head_cols)
    grad_queries = jnp.concatenate([entry[1] for entry in results], axis=-1).reshape(SEGS, SEG_LEN, KV_HEADS * head_cols)
    grad_keys = jnp.concatenate([entry[2] for entry in results], axis=-1).reshape(SEGS, SEG_LEN, KV_HEADS * HEAD_DIM)
    grad_values = jnp.concatenate([entry[3] for entry in results], axis=-1).reshape(SEGS, SEG_LEN, KV_HEADS * HEAD_DIM)
    prompt_key_total = jnp.concatenate([jnp.sum(entry[4], axis=0) for entry in results], axis=-1)
    prompt_value_total = jnp.concatenate([jnp.sum(entry[5], axis=0) for entry in results], axis=-1)
    prompt_grads = jnp.stack([prompt_key_total, prompt_value_total])
    return attended, grad_queries, grad_keys, grad_values, prompt_grads
```

```python
import functools

import jax
import jax.numpy as jnp
from jax import lax
from jax.experimental import pallas as pl
from jax.experimental.pallas import tpu as pltpu
from jax.sharding import PartitionSpec as P

LINE = ("seq", "rep")
NT = (((1,), (1,)), ((), ()))
NN = (((1,), (0,)), ((), ()))
LOG2E = 1.4426950408889634
VMEM = pl.BlockSpec(memory_space=pltpu.VMEM)
SMEM = pl.BlockSpec(memory_space=pltpu.SMEM)
PARAMS = pltpu.CompilerParams(vmem_limit_bytes=56 * 1024 * 1024)


def dot(left, right, dims):
    return lax.dot_general(left, right, dims, preferred_element_type=jnp.float32)


def pack_kernel(band, piece, q_ref, k_ref, v_ref, g_ref, pk_ref, pv_ref, out_ref):
    core = lax.axis_index("rep")
    devices = out_ref.shape[0]
    head_size = k_ref.shape[2]
    for dest in range(devices):
        start = pl.multiple_of((dest % 2) * 2 * piece + core * piece, 16)
        out_ref[dest, :piece, :] = pk_ref[pl.ds(start, piece), :]
        out_ref[dest, piece : 2 * piece, :] = pv_ref[pl.ds(start, piece), :]
        row = 2 * piece
        for source in (k_ref, v_ref, q_ref, g_ref):
            for tile in range(source.shape[2] // head_size):
                for slot in range(source.shape[0]):
                    out_ref[dest, row : row + band, :] = source[
                        slot, dest * band : (dest + 1) * band, tile * head_size : (tile + 1) * head_size
                    ]
                    row += band


def pack_plain(band, piece, q, k, v, g, pk, pv):
    slots, length, head_size = k.shape
    devices = length // band
    rows = jnp.concatenate([k, v, q, g], axis=2)
    tiles = rows.shape[2] // head_size
    rows = rows.reshape(slots, devices, band, tiles, head_size).transpose(1, 3, 0, 2, 4)
    rows = rows.reshape(devices, tiles * slots * band, head_size)
    core = lax.axis_index("rep")
    quarters = jnp.stack([pk, pv]).reshape(2, 2, 2, piece, head_size)
    quarters = lax.dynamic_index_in_dim(quarters, core, 2, keepdims=False)
    quarters = quarters.transpose(1, 0, 2, 3).reshape(2, 2 * piece, head_size)
    quarters = jnp.broadcast_to(quarters[None], (devices // 2, 2, 2 * piece, head_size))
    return jnp.concatenate([quarters.reshape(devices, 2 * piece, head_size), rows], axis=1)


def pick_kernel(band, skip, tiles, packing_ref, in_ref, out_ref):
    slots = 2
    for target in range(out_ref.shape[0] * slots):
        chosen = packing_ref[target]
        device = chosen // slots
        slot = chosen % slots
        for tile in range(tiles):
            out_ref[target // slots, tile * slots + target % slots] = in_ref[device, skip + tile * slots + slot]


def attend_kernel(
    band, piece, heads, natural, length_ref, tree_ref, rows_ref, own_ref, other_ref,
    att_ref, gq_ref, gk_ref, gv_ref, keep_ref, send_ref, keys, values, key_acc, value_acc,
):
    core = lax.axis_index("rep")
    head_size = rows_ref.shape[2]
    blocks = rows_ref.shape[0]
    high = rows_ref.shape[1] // (2 + 2 * heads)
    rows = blocks * high
    seg_length = rows // 2
    prompt = keys.shape[0] - rows
    scale = head_size ** (-0.5)

    def tile_of(index):
        return rows_ref[:, index * high : (index + 1) * high, :].reshape(rows, head_size)

    for source in range(own_ref.shape[0]):
        base = (source // 2) * 4 * piece + (source % 2) * piece
        for ref, half in ((own_ref, core), (other_ref, 1 - core)):
            start = pl.multiple_of(base + half * 2 * piece, 16)
            keys[pl.ds(start, piece), :] = ref[source, :piece, :]
            values[pl.ds(start, piece), :] = ref[source, piece:, :]
    keys[prompt:, :] = tile_of(0)
    values[prompt:, :] = tile_of(1)

    def place(shape, axis):
        index = lax.broadcasted_iota(jnp.int32, shape, axis)
        slot = (index % (2 * band)) // band
        return slot, (index // (2 * band)) * band + index % band

    row_slot, row_at = place((rows, rows), 0)
    col_slot, col_at = place((rows, rows), 1)
    first, second = length_ref[0], length_ref[1]
    tree = jnp.where(
        row_slot == 0,
        jnp.where(col_slot == 0, tree_ref[0, 0], tree_ref[0, 1]),
        jnp.where(col_slot == 0, tree_ref[1, 0], tree_ref[1, 1]),
    )
    visible = (
        (tree == 1)
        & (col_at < jnp.where(col_slot == 0, first, second))
        & ((row_slot != col_slot) | (col_at <= row_at))
    )
    slot, at = place((rows, head_size), 0)
    live = (at < jnp.where(slot == 0, first, second)).astype(jnp.float32)
    live_bf = live.astype(jnp.bfloat16)
    all_keys = keys[...]
    all_values = values[...]

    def put(ref, value, column):
        if natural:
            for block in range(blocks):
                for one in range(2):
                    start = block * high + one * band
                    ref[one, block * band : (block + 1) * band, column * head_size : (column + 1) * head_size] = value[
                        start : start + band, :
                    ]
        else:
            ref[column] = value

    for head in range(heads):
        query = tile_of(2 + head)
        grad = tile_of(2 + heads + head) * live_bf
        scores = dot(query, all_keys, NT)
        prompt_scores = scores[:, :prompt]
        tree_scores = jnp.where(visible, scores[:, prompt:], -1e30)
        top = jnp.maximum(
            jnp.max(prompt_scores, axis=1, keepdims=True), jnp.max(tree_scores, axis=1, keepdims=True)
        )
        scores = jnp.concatenate([prompt_scores, tree_scores], axis=1)
        powers = jnp.exp2((scores - top) * (scale * LOG2E))
        probs = powers * (1.0 / jnp.sum(powers, axis=1, keepdims=True))
        probs_b = probs.astype(jnp.bfloat16)
        attended = (dot(probs_b, all_values, NN) * live).astype(jnp.bfloat16)
        put(att_ref, attended, head)
        delta = jnp.sum(grad.astype(jnp.float32) * attended.astype(jnp.float32), axis=1, keepdims=True)
        dscore = (probs * (dot(grad, all_values, NT) - delta)).astype(jnp.bfloat16)
        put(gq_ref, (dot(dscore, all_keys, NN) * scale).astype(jnp.bfloat16), head)
        key_part = dot(query.T, dscore, NN)
        value_part = dot(grad.T, probs_b, NN)
        if head == 0:
            key_acc[...] = key_part
            value_acc[...] = value_part
        else:
            key_acc[...] += key_part
            value_acc[...] += value_part
    put(gk_ref, (key_acc[:, prompt:] * scale).T.astype(jnp.bfloat16), 0)
    put(gv_ref, value_acc[:, prompt:].T.astype(jnp.bfloat16), 0)

    @pl.when(core == 0)
    def _():
        keep_ref[...] = key_acc[:, :prompt] * scale
        send_ref[...] = value_acc[:, :prompt]

    @pl.when(core != 0)
    def _():
        keep_ref[...] = value_acc[:, :prompt]
        send_ref[...] = key_acc[:, :prompt] * scale


def swap_cores(value):
    return lax.ppermute(value, "rep", [(0, 1), (1, 0)])


def per_device(
    queries, response_keys, response_values, grad_out, prompt_keys, prompt_values, packing, lengths, tree_mask
):
    slots, seg_length, head_size = response_keys.shape
    heads = queries.shape[2] // head_size
    tiles = 2 + 2 * heads
    chips = lax.axis_size("seq")
    devices = chips * lax.axis_size("rep")
    band = seg_length // devices
    share = prompt_keys.shape[0]
    piece = share // 4
    prompt = share * chips
    rows = slots * seg_length
    natural = band % 16 == 0
    bf16 = jnp.bfloat16

    sources = (queries, response_keys, response_values, grad_out, prompt_keys, prompt_values)
    message_rows = 2 * piece + tiles * slots * band
    if natural:
        message = pl.pallas_call(
            functools.partial(pack_kernel, band, piece),
            out_shape=jax.ShapeDtypeStruct((devices, message_rows, head_size), bf16),
            in_specs=[VMEM] * 6,
            out_specs=VMEM,
            compiler_params=PARAMS,
            name="pack",
        )(*sources)
    else:
        message = pack_plain(band, piece, *sources)
    banded = lax.all_to_all(message, LINE, split_axis=0, concat_axis=0)
    prompt_own = banded[:, : 2 * piece, :]
    prompt_other = swap_cores(prompt_own)
    if natural:
        picked = pl.pallas_call(
            functools.partial(pick_kernel, band, 2 * piece // band, tiles),
            out_shape=jax.ShapeDtypeStruct((devices, tiles * slots, band, head_size), bf16),
            in_specs=[SMEM, VMEM],
            out_specs=VMEM,
            compiler_params=PARAMS,
            name="pick",
        )(packing, banded.reshape(devices, message_rows // band, band, head_size))
        moved = lax.all_to_all(picked, LINE, split_axis=0, concat_axis=0)
        moved = moved.reshape(devices, tiles * slots * band, head_size)
    else:
        held = banded[:, 2 * piece :, :].reshape(devices, tiles, slots, band, head_size)
        held = held.transpose(0, 2, 1, 3, 4).reshape(devices * slots, tiles, band, head_size)
        picked = jnp.take(held, packing, axis=0).reshape(devices, slots, tiles, band, head_size)
        moved = lax.all_to_all(picked, LINE, split_axis=0, concat_axis=0)
        moved = moved.transpose(2, 0, 1, 3, 4).reshape(1, tiles * rows, head_size)

    if natural:
        wide, narrow = (slots, seg_length, heads * head_size), (slots, seg_length, head_size)
    else:
        wide, narrow = (heads, rows, head_size), (1, rows, head_size)
    attended, grad_queries, grad_keys, grad_values, keep, send = pl.pallas_call(
        functools.partial(attend_kernel, band, piece, heads, natural),
        out_shape=[
            jax.ShapeDtypeStruct(wide, bf16),
            jax.ShapeDtypeStruct(wide, bf16),
            jax.ShapeDtypeStruct(narrow, bf16),
            jax.ShapeDtypeStruct(narrow, bf16),
            jax.ShapeDtypeStruct((head_size, prompt), jnp.float32),
            jax.ShapeDtypeStruct((head_size, prompt), jnp.float32),
        ],
        in_specs=[SMEM, SMEM, VMEM, VMEM, VMEM],
        out_specs=[VMEM] * 6,
        scratch_shapes=[
            pltpu.VMEM((prompt + rows, head_size), bf16),
            pltpu.VMEM((prompt + rows, head_size), bf16),
            pltpu.VMEM((head_size, prompt + rows), jnp.float32),
            pltpu.VMEM((head_size, prompt + rows), jnp.float32),
        ],
        compiler_params=PARAMS,
        name="attend",
    )(lengths, tree_mask, moved, prompt_own, prompt_other)
    if not natural:

        def restore(value):
            value = value.reshape(-1, devices, slots, band, head_size).transpose(2, 1, 3, 0, 4)
            return value.reshape(slots, seg_length, -1)

        attended, grad_queries, grad_keys, grad_values = (
            restore(value) for value in (attended, grad_queries, grad_keys, grad_values)
        )

    total = keep + swap_cores(send)
    parts = total.reshape(head_size, chips, share).transpose(1, 0, 2).astype(bf16)
    gathered = lax.all_to_all(parts, "seq", split_axis=0, concat_axis=0)
    own = jnp.sum(gathered.astype(jnp.float32), axis=0).T
    other = swap_cores(own)
    core = lax.axis_index("rep")
    prompt_grads = jnp.stack([jnp.where(core == 0, own, other), jnp.where(core == 0, other, own)])
    return attended, grad_queries, grad_keys, grad_values, prompt_grads


def solution(mesh):
    segments = P(("groups", "seq", "rep"), None, "head")
    in_specs = (
        segments,
        segments,
        segments,
        segments,
        P(("groups", "seq"), "head"),
        P(("groups", "seq"), "head"),
        P("groups"),
        P(("groups", "seq", "rep")),
        P(("groups", "seq", "rep"), None),
    )
    out_specs = (segments, segments, segments, segments, P(None, ("groups", "seq"), "head"))
    return jax.shard_map(per_device, mesh=mesh, in_specs=in_specs, out_specs=out_specs, check_vma=False)
```

```python
import functools

import jax
import jax.numpy as jnp
from jax import lax
from jax.experimental import pallas as pl
from jax.experimental.pallas import tpu as pltpu
from jax.sharding import PartitionSpec as P

NT = (((1,), (1,)), ((), ()))
NN = (((1,), (0,)), ((), ()))
LOG2E = 1.4426950408889634
SPLIT = (5,)
VMEM = pl.BlockSpec(memory_space=pltpu.VMEM)
SMEM = pl.BlockSpec(memory_space=pltpu.SMEM)
SMALL = pltpu.CompilerParams(vmem_limit_bytes=8 * 1024 * 1024)
LARGE = pltpu.CompilerParams(vmem_limit_bytes=36 * 1024 * 1024)


def dot(left, right, dims):
    return lax.dot_general(left, right, dims, preferred_element_type=jnp.float32)


def chunk_tiles(split):
    chunks, head = [], 0
    for count in split:
        part = [(0, 0), (1, 0)] if head == 0 else []
        part += [(2, one) for one in range(head, head + count)] + [(3, one) for one in range(head, head + count)]
        chunks.append(part)
        head += count
    return chunks


def pack_kernel(band, chunks, k_ref, v_ref, q_ref, g_ref, *outs):
    me = lax.axis_index("seq")
    sources = (k_ref, v_ref, q_ref, g_ref)
    size = k_ref.shape[2]
    chips = len(outs) // len(chunks)
    for number, chunk in enumerate(chunks):
        for far in range(chips):
            out = outs[number * chips + far]
            start = pl.multiple_of((me ^ far) * band, 16)
            row = 0
            for source, tile in chunk:
                for slot in range(k_ref.shape[0]):
                    out[row : row + band, :] = sources[source][
                        slot, pl.ds(start, band), tile * size : (tile + 1) * size
                    ]
                    row += band


def pick_kernel(band, chips, packing_ref, *refs):
    pieces, outs, held = refs[: 2 * chips], refs[2 * chips : 3 * chips], refs[3 * chips]
    me = lax.axis_index("seq")
    core = lax.axis_index("rep")
    for number, piece in enumerate(pieces):
        held[number] = piece[...]
    tiles = outs[0].shape[0] // (2 * band)
    for far in range(chips):
        for slot in range(2):
            chosen = packing_ref[((me ^ far) * 2 + core) * 2 + slot]
            device = chosen // 2
            number = ((device // 2) ^ me) + chips * ((device % 2) ^ core)
            for tile in range(tiles):
                start = pl.multiple_of(tile * 2 * band + (chosen % 2) * band, 16)
                row = tile * 2 * band + slot * band
                outs[far][row : row + band, :] = held[number, pl.ds(start, band), :]


def attend_kernel(
    band, heads, head_from, last, xor, natural, own_count, row_count, length_ref, tree_ref, *refs
):
    refs = list(refs)

    def take(count):
        taken = refs[:count]
        del refs[:count]
        return taken

    first = head_from == 0
    key_rows = take(row_count)
    head_rows = key_rows if first else take(row_count)
    own_refs, other_refs = take(own_count), take(own_count)
    before = [] if first else take(4)
    att_ref, gq_ref = take(2)
    results = take(4 if last else 2)
    keys, values, key_acc, value_acc = take(4)
    core = lax.axis_index("rep")
    me = lax.axis_index("seq") if xor else 0
    size = key_rows[0].shape[1]
    high = 2 * band if xor else key_acc.shape[1] - sum(ref.shape[0] for ref in own_refs)
    rows = high * row_count
    prompt = keys.shape[0] - rows
    share = prompt // own_count
    scale = size ** (-0.5)

    def tile_of(source, index):
        parts = [ref[index * high : (index + 1) * high, :] for ref in source]
        return parts[0] if len(parts) == 1 else jnp.concatenate(parts, axis=0)

    @pl.when(core == 0)
    def _():
        for number in range(own_count):
            keys[number * share : (number + 1) * share, :] = own_refs[number][...]
            values[number * share : (number + 1) * share, :] = other_refs[number][...]

    @pl.when(core != 0)
    def _():
        for number in range(own_count):
            keys[number * share : (number + 1) * share, :] = other_refs[number][...]
            values[number * share : (number + 1) * share, :] = own_refs[number][...]

    keys[prompt:, :] = tile_of(key_rows, 0)
    values[prompt:, :] = tile_of(key_rows, 1)

    def place(shape, axis):
        index = lax.broadcasted_iota(jnp.int32, shape, axis)
        slot = (index % (2 * band)) // band
        return slot, ((index // (2 * band)) ^ me) * band + index % band

    row_slot, row_at = place((rows, rows), 0)
    col_slot, col_at = place((rows, rows), 1)
    length_a, length_b = length_ref[0], length_ref[1]
    tree = jnp.where(
        row_slot == 0,
        jnp.where(col_slot == 0, tree_ref[0, 0], tree_ref[0, 1]),
        jnp.where(col_slot == 0, tree_ref[1, 0], tree_ref[1, 1]),
    )
    visible = (
        (tree == 1)
        & (col_at < jnp.where(col_slot == 0, length_a, length_b))
        & ((row_slot != col_slot) | (col_at <= row_at))
    )
    slot, at = place((rows, size), 0)
    live = (at < jnp.where(slot == 0, length_a, length_b)).astype(jnp.float32)
    live_bf = live.astype(jnp.bfloat16)
    all_keys = keys[...]
    all_values = values[...]

    def put(ref, value, column):
        if natural:
            for number in range(row_count):
                for one in range(2):
                    start = number * high + one * band
                    at = pl.multiple_of((number ^ me) * band, 16)
                    ref[one, pl.ds(at, band), column * size : (column + 1) * size] = value[start : start + band, :]
        else:
            ref[column] = value

    if not first:
        if natural:
            att_ref[:, :, : head_from * size] = before[0][...]
            gq_ref[:, :, : head_from * size] = before[1][...]
        else:
            att_ref[:head_from] = before[0][...]
            gq_ref[:head_from] = before[1][...]
    for head in range(heads):
        offset = 2 if first else 0
        query = tile_of(head_rows, offset + head)
        grad = tile_of(head_rows, offset + heads + head) * live_bf
        scores = dot(query, all_keys, NT)
        prompt_scores = scores[:, :prompt]
        tree_scores = jnp.where(visible, scores[:, prompt:], -1e30)
        top = jnp.maximum(
            jnp.max(prompt_scores, axis=1, keepdims=True), jnp.max(tree_scores, axis=1, keepdims=True)
        )
        scores = jnp.concatenate([prompt_scores, tree_scores], axis=1)
        powers = jnp.exp2((scores - top) * (scale * LOG2E))
        probs = powers * (1.0 / jnp.sum(powers, axis=1, keepdims=True))
        probs_b = probs.astype(jnp.bfloat16)
        attended = (dot(probs_b, all_values, NN) * live).astype(jnp.bfloat16)
        put(att_ref, attended, head_from + head)
        delta = jnp.sum(grad.astype(jnp.float32) * attended.astype(jnp.float32), axis=1, keepdims=True)
        dscore = (probs * (dot(grad, all_values, NT) - delta)).astype(jnp.bfloat16)
        put(gq_ref, (dot(dscore, all_keys, NN) * scale).astype(jnp.bfloat16), head_from + head)
        key_part = dot(query.T, dscore, NN)
        value_part = dot(grad.T, probs_b, NN)
        if head == 0 and first:
            key_acc[...] = key_part
            value_acc[...] = value_part
        elif head == 0:
            key_acc[...] = before[2][...] + key_part
            value_acc[...] = before[3][...] + value_part
        else:
            key_acc[...] += key_part
            value_acc[...] += value_part
    if not last:
        results[0][...] = key_acc[...]
        results[1][...] = value_acc[...]
        return
    gk_ref, gv_ref, keep_ref, send_ref = results
    put(gk_ref, (key_acc[:, prompt:] * scale).T.astype(jnp.bfloat16), 0)
    put(gv_ref, value_acc[:, prompt:].T.astype(jnp.bfloat16), 0)

    @pl.when(core == 0)
    def _():
        for number in range(own_count):
            keep_ref[number] = key_acc[:, number * share : (number + 1) * share] * scale
            send_ref[number] = value_acc[:, number * share : (number + 1) * share]

    @pl.when(core != 0)
    def _():
        for number in range(own_count):
            keep_ref[number] = value_acc[:, number * share : (number + 1) * share]
            send_ref[number] = key_acc[:, number * share : (number + 1) * share] * scale


def swap_cores(value):
    return lax.ppermute(value, "rep", [(0, 1), (1, 0)])


def to_far(value, far):
    return lax.ppermute(value, "seq", [(chip, chip ^ far) for chip in range(lax.axis_size("seq"))])


def spread(parts):
    order = sorted(range(1, len(parts)), key=lambda far: -(far & 2) - (far == 3))
    got = {far: to_far(parts[far], far) for far in order}
    return [parts[0]] + [got[far] for far in range(1, len(parts))]


def per_device(
    queries, response_keys, response_values, grad_out, prompt_keys, prompt_values, packing, lengths, tree_mask
):
    slots, seg_length, size = response_keys.shape
    heads = queries.shape[2] // size
    chips = lax.axis_size("seq")
    band = seg_length // chips
    share = prompt_keys.shape[0]
    prompt = share * chips
    rows = slots * seg_length
    core = lax.axis_index("rep")
    xor = band % 16 == 0 and chips in (2, 4, 8)
    natural = xor
    bf16 = jnp.bfloat16
    split = SPLIT if sum(SPLIT) == heads else (heads,)
    chunks = chunk_tiles(split)
    sources = (response_keys, response_values, queries, grad_out)

    prompt_mine = jnp.where(core == 0, prompt_keys, prompt_values)
    if xor:
        packed = pl.pallas_call(
            functools.partial(pack_kernel, band, chunks),
            out_shape=[
                jax.ShapeDtypeStruct((len(chunk) * slots * band, size), bf16) for chunk in chunks for _ in range(chips)
            ],
            in_specs=[VMEM] * 4,
            out_specs=[VMEM] * (chips * len(chunks)),
            compiler_params=SMALL,
            name="pack",
        )(*sources)
        rows_in = []
        for number, chunk in enumerate(chunks):
            mine = spread(packed[number * chips : (number + 1) * chips])
            theirs = [swap_cores(piece) for piece in mine]
            picked = pl.pallas_call(
                functools.partial(pick_kernel, band, chips),
                out_shape=[jax.ShapeDtypeStruct((len(chunk) * slots * band, size), bf16)] * chips,
                in_specs=[SMEM] + [VMEM] * (2 * chips),
                out_specs=[VMEM] * chips,
                scratch_shapes=[pltpu.VMEM((2 * chips, len(chunk) * slots * band, size), bf16)],
                compiler_params=SMALL,
                name="pick",
            )(packing, *mine, *theirs)
            rows_in.append(spread(picked))
        prompt_own = spread([prompt_mine] * chips)
        prompt_other = [swap_cores(piece) for piece in prompt_own]
    else:
        rows_in = []
        for chunk in chunks:
            tiles = [sources[source][:, :, tile * size : (tile + 1) * size] for source, tile in chunk]
            piece = jnp.stack(tiles, axis=2).reshape(slots, chips, band, len(chunk), size).transpose(1, 0, 3, 2, 4)
            mine = lax.all_to_all(piece, "seq", split_axis=0, concat_axis=0)
            theirs = swap_cores(mine)
            both = jnp.stack([jnp.where(core == 0, mine, theirs), jnp.where(core == 0, theirs, mine)], axis=1)
            both = both.reshape(chips * 2 * slots, len(chunk), band, size)
            wanted = packing.reshape(chips, 2, slots)
            wanted = lax.dynamic_index_in_dim(wanted, core, 1, keepdims=False)
            picked = jnp.take(both, wanted.reshape(-1), axis=0).reshape(chips, slots, len(chunk), band, size)
            moved = lax.all_to_all(picked, "seq", split_axis=0, concat_axis=0)
            rows_in.append([moved.transpose(2, 0, 1, 3, 4).reshape(len(chunk) * rows, size)])
        prompt_own = [lax.all_gather(prompt_mine, "seq", axis=0, tiled=True)]
        prompt_other = [swap_cores(prompt_own[0])]

    carried = []
    own_count, row_count = len(prompt_own), len(rows_in[0])
    head_from = 0
    for number, count in enumerate(split):
        last = number == len(split) - 1
        done = head_from + count
        wide = (slots, seg_length, done * size) if natural else (done, rows, size)
        narrow = (slots, seg_length, size) if natural else (1, rows, size)
        out_shape = [jax.ShapeDtypeStruct(wide, bf16)] * 2
        if last:
            out_shape += [jax.ShapeDtypeStruct(narrow, bf16)] * 2
            out_shape += [jax.ShapeDtypeStruct((own_count, size, prompt // own_count), jnp.float32)] * 2
        else:
            out_shape += [jax.ShapeDtypeStruct((size, prompt + rows), jnp.float32)] * 2
        operands = [*rows_in[0], *(rows_in[number] if number else []), *prompt_own, *prompt_other, *carried]
        work = 2 * 6 * count * rows * (prompt + rows) * size
        carried = pl.pallas_call(
            functools.partial(attend_kernel, band, count, head_from, last, xor, natural, own_count, row_count),
            out_shape=out_shape,
            in_specs=[SMEM, SMEM] + [VMEM] * len(operands),
            out_specs=[VMEM] * len(out_shape),
            scratch_shapes=[
                pltpu.VMEM((prompt + rows, size), bf16),
                pltpu.VMEM((prompt + rows, size), bf16),
                pltpu.VMEM((size, prompt + rows), jnp.float32),
                pltpu.VMEM((size, prompt + rows), jnp.float32),
            ],
            compiler_params=LARGE,
            cost_estimate=pl.CostEstimate(
                flops=2 * work, bytes_accessed=1 << 20, transcendentals=count * rows * (prompt + rows)
            ),
            name="attend",
        )(lengths, tree_mask, *operands)
        head_from = done
    attended, grad_queries, grad_keys, grad_values, keep, send = carried
    if not natural:

        def restore(value):
            value = value.reshape(-1, chips, slots, band, size).transpose(2, 1, 3, 0, 4)
            return value.reshape(slots, seg_length, -1)

        attended, grad_queries, grad_keys, grad_values = (
            restore(value) for value in (attended, grad_queries, grad_keys, grad_values)
        )

    received = swap_cores(send)
    if xor:
        total = [keep[number] + received[number] for number in range(chips)]
        arrived = spread([total[0]] + [part.astype(bf16) for part in total[1:]])
        own = sum(part.astype(jnp.float32) for part in arrived).T
    else:
        total = (keep + received).reshape(size, chips, share).transpose(1, 0, 2).astype(bf16)
        arrived = lax.all_to_all(total, "seq", split_axis=0, concat_axis=0)
        own = jnp.sum(arrived.astype(jnp.float32), axis=0).T
    other = swap_cores(own)
    prompt_grads = jnp.stack([jnp.where(core == 0, own, other), jnp.where(core == 0, other, own)])
    return attended, grad_queries, grad_keys, grad_values, prompt_grads


def solution(mesh):
    segments = P(("groups", "seq", "rep"), None, "head")
    in_specs = (
        segments,
        segments,
        segments,
        segments,
        P(("groups", "seq"), "head"),
        P(("groups", "seq"), "head"),
        P("groups"),
        P(("groups", "seq", "rep")),
        P(("groups", "seq", "rep"), None),
    )
    out_specs = (segments, segments, segments, segments, P(None, ("groups", "seq"), "head"))
    return jax.shard_map(per_device, mesh=mesh, in_specs=in_specs, out_specs=out_specs, check_vma=False)
```

```python
import functools

import jax
import jax.numpy as jnp
from jax import lax
from jax.experimental import pallas as pl
from jax.experimental.pallas import tpu as pltpu
from jax.sharding import PartitionSpec as P

NT = (((1,), (1,)), ((), ()))
NN = (((1,), (0,)), ((), ()))
LOG2E = 1.4426950408889634
GROUPS = (5,)
VMEM = pl.BlockSpec(memory_space=pltpu.VMEM)
HBM = pl.BlockSpec(memory_space=pltpu.HBM)
SMEM = pl.BlockSpec(memory_space=pltpu.SMEM)
SMALL = pltpu.CompilerParams(vmem_limit_bytes=8 * 1024 * 1024)
FULL = pltpu.CompilerParams(vmem_limit_bytes=56 * 1024 * 1024)
LARGE = pltpu.CompilerParams(vmem_limit_bytes=36 * 1024 * 1024)


def dot(left, right, dims):
    return lax.dot_general(left, right, dims, preferred_element_type=jnp.float32)


def pack_kernel(band, tiles, k_hbm, v_hbm, q_hbm, g_hbm, pk_hbm, pv_hbm, *refs):
    chips = len(refs) - 5
    outs, held, sems = refs[:chips], refs[chips:-1], refs[-1]
    me = lax.axis_index("seq")
    core = lax.axis_index("rep")
    share, size = pk_hbm.shape
    rows = len(tiles) * 2 * band
    targets = [out.at[pl.ds(rows, share), :] for out in outs[:3]]
    copies = [
        pltpu.make_async_copy(source, target, sems.at[number])
        for number, (source, target) in enumerate(zip((k_hbm, v_hbm, q_hbm, g_hbm), held))
    ]
    for copy in copies:
        copy.start()

    def prompt_copies(source):
        return [pltpu.make_async_copy(source, target, sems.at[4 + far]) for far, target in enumerate(targets)]

    @pl.when(core == 0)
    def _():
        for copy in prompt_copies(pk_hbm):
            copy.start()

    @pl.when(core != 0)
    def _():
        for copy in prompt_copies(pv_hbm):
            copy.start()

    for copy in copies:
        copy.wait()
    for far, out in enumerate(outs):
        start = pl.multiple_of((me ^ far) * band, 16)
        row = 0
        for source, tile in tiles:
            for slot in range(2):
                out[row : row + band, :] = held[source][slot, pl.ds(start, band), tile * size : (tile + 1) * size]
                row += band
    for copy in prompt_copies(pk_hbm):
        copy.wait()


def pick_kernel(band, chips, counts, wanted_ref, *refs):
    pieces, outs, held = refs[: 2 * chips], refs[2 * chips : -1], refs[-1]
    me = lax.axis_index("seq")
    core = lax.axis_index("rep")
    for number, piece in enumerate(pieces):
        held[number] = piece[: held.shape[1], :]
    start = 2 * 2 * band
    for piece in (pieces[2], pieces[chips + 2]):
        passed = piece[held.shape[1] :, :]
        outs[1][start : start + passed.shape[0], :] = passed
        start += passed.shape[0]
    for far in range(chips):
        for slot in range(2):
            chosen = wanted_ref[me ^ far, slot]
            device = chosen // 2
            number = ((device // 2) ^ me) + chips * ((device % 2) ^ core)
            tile = 0
            for chunk, count in enumerate(counts):
                out = outs[chunk * chips + far]
                for one in range(count):
                    start = pl.multiple_of(tile * 2 * band + (chosen % 2) * band, 16)
                    row = one * 2 * band + slot * band
                    out[row : row + band, :] = held[number, pl.ds(start, band), :]
                    tile += 1


def combine_kernel(keep_ref, received_ref, *outs):
    for number, out in enumerate(outs):
        out[...] = (keep_ref[number] + received_ref[number].astype(jnp.float32)).astype(out.dtype)


def finish_kernel(*refs):
    mine, theirs, out_ref = refs[: len(refs) // 2], refs[len(refs) // 2 : -1], refs[-1]
    core = lax.axis_index("rep")
    for parts, place in ((mine, core), (theirs, 1 - core)):
        total = parts[0][...]
        for part in parts[1:]:
            total = total + part[...].astype(jnp.float32)
        out_ref[place] = total.T


def attend_kernel(band, heads, total_rows, bands, first, last, xor, row_count, length_ref, tree_ref, *refs):
    refs = list(refs)

    def take(count):
        taken = refs[:count]
        del refs[:count]
        return taken

    head_rows = take(len(bands))
    if first:
        pair_rows = take(row_count)
        own_parts, other_parts = take(3 if xor else 1), take(3 if xor else 1)
    else:
        keys, values, att_before, gq_before, key_before, value_before = take(6)
    att_ref, gq_ref = take(2)
    if first:
        keys, values = (refs.pop(-2), refs.pop(-1)) if last else take(2)
    core = lax.axis_index("rep")
    me = lax.axis_index("seq") if xor else 0
    size = keys.shape[1]
    prompt = keys.shape[0] - total_rows
    share = prompt // row_count
    high = total_rows // row_count
    rows = high * len(bands)
    scale = size ** (-0.5)

    def fill(keys_of, values_of):
        for target, pieces in ((keys, keys_of), (values, values_of)):
            for number, (piece, start) in enumerate(pieces):
                target[number * share : (number + 1) * share, :] = piece[start : start + share, :]

    if first:
        own_parts, other_parts = (
            [(piece, piece.shape[0] - share) for piece in parts] for parts in (own_parts, other_parts)
        )
        if xor:
            own_parts.append((pair_rows[1], 2 * high))
            other_parts.append((pair_rows[1], 2 * high + share))

        @pl.when(core == 0)
        def _():
            fill(own_parts, other_parts)

        @pl.when(core != 0)
        def _():
            fill(other_parts, own_parts)

        for number, pair in enumerate(pair_rows):
            start = prompt + number * high
            keys[start : start + high, :] = pair[:high, :]
            values[start : start + high, :] = pair[high : 2 * high, :]

    def place(shape, axis, start):
        index = lax.broadcasted_iota(jnp.int32, shape, axis) + start
        slot = (index % (2 * band)) // band
        return slot, ((index // (2 * band)) ^ me) * band + index % band

    length_a, length_b = length_ref[0], length_ref[1]
    row_slot, row_at = place((rows, total_rows), 0, bands[0] * high)
    col_slot, col_at = place((rows, total_rows), 1, 0)
    tree = jnp.where(
        row_slot == 0,
        jnp.where(col_slot == 0, tree_ref[0, 0], tree_ref[0, 1]),
        jnp.where(col_slot == 0, tree_ref[1, 0], tree_ref[1, 1]),
    )
    visible = (
        (tree == 1)
        & (col_at < jnp.where(col_slot == 0, length_a, length_b))
        & ((row_slot != col_slot) | (col_at <= row_at))
    )
    slot, at = place((rows, size), 0, bands[0] * high)
    live = (at < jnp.where(slot == 0, length_a, length_b)).astype(jnp.float32)
    live_bf = live.astype(jnp.bfloat16)
    all_keys = keys[...]
    all_values = values[...]

    def put(ref, value, head, placed):
        if not xor:
            ref[head] = value
            return
        for number, which in enumerate(placed):
            for one in range(2):
                start = number * high + one * band
                at = pl.multiple_of((which ^ me) * band, 16)
                ref[one, pl.ds(at, band), head * size : (head + 1) * size] = value[start : start + band, :]

    def rows_of(index):
        parts = [ref[index * high : (index + 1) * high, :] for ref in head_rows]
        return parts[0] if len(parts) == 1 else jnp.concatenate(parts, axis=0)

    key_total, value_total = (None, None) if first else (key_before[...], value_before[...])
    start = 0
    for count in GROUPS if sum(GROUPS) == heads else (heads,):
        query = jnp.concatenate([rows_of(start + head) for head in range(count)], axis=0)
        grad = jnp.concatenate([rows_of(heads + start + head) * live_bf for head in range(count)], axis=0)
        scores = dot(query, all_keys, NT)
        prompt_scores = scores[:, :prompt]
        tree_scores = jnp.concatenate(
            [jnp.where(visible, scores[head * rows : (head + 1) * rows, prompt:], -1e30) for head in range(count)],
            axis=0,
        )
        top = jnp.maximum(
            jnp.max(prompt_scores, axis=1, keepdims=True), jnp.max(tree_scores, axis=1, keepdims=True)
        )
        scores = jnp.concatenate([prompt_scores, tree_scores], axis=1)
        powers = jnp.exp2((scores - top) * (scale * LOG2E))
        probs = powers * (1.0 / jnp.sum(powers, axis=1, keepdims=True))
        probs_b = probs.astype(jnp.bfloat16)
        attended = dot(probs_b, all_values, NN)
        attended = jnp.concatenate(
            [(attended[head * rows : (head + 1) * rows] * live).astype(jnp.bfloat16) for head in range(count)], axis=0
        )
        delta = jnp.sum(grad.astype(jnp.float32) * attended.astype(jnp.float32), axis=1, keepdims=True)
        dscore = (probs * (dot(grad, all_values, NT) - delta)).astype(jnp.bfloat16)
        grad_query = (dot(dscore, all_keys, NN) * scale).astype(jnp.bfloat16)
        key_part = dot(query.T, dscore, NN)
        value_part = dot(grad.T, probs_b, NN)
        key_total = key_part if key_total is None else key_total + key_part
        value_total = value_part if value_total is None else value_total + value_part
        for head in range(count):
            for ref, result in ((att_ref, attended), (gq_ref, grad_query)):
                result = result[head * rows : (head + 1) * rows, :]
                if last:
                    put(ref, result, start + head, bands)
                else:
                    ref[start + head] = result
        start += count
    if not last:
        refs[0][...] = key_total
        refs[1][...] = value_total
        return
    if not first:
        for head in range(heads):
            for ref, before in ((att_ref, att_before), (gq_ref, gq_before)):
                put(ref, before[head], head, range(bands[0]))
    gk_ref, gv_ref, keep_ref, send_ref = refs
    for ref, result in ((gk_ref, key_total[:, prompt:] * scale), (gv_ref, value_total[:, prompt:])):
        put(ref, result.T.astype(jnp.bfloat16), 0, range(row_count))

    def fill_sums(key_ref, value_ref):
        for number in range(row_count):
            part = slice(number * share, (number + 1) * share)
            key_ref[number] = (key_total[:, part] * scale).astype(key_ref.dtype)
            value_ref[number] = value_total[:, part].astype(value_ref.dtype)

    @pl.when(core == 0)
    def _():
        fill_sums(keep_ref, send_ref)

    @pl.when(core != 0)
    def _():
        fill_sums(send_ref, keep_ref)


def combine_kernel(keep_ref, received_ref, *outs):
    for number, out in enumerate(outs):
        out[...] = (keep_ref[number] + received_ref[number].astype(jnp.float32)).astype(out.dtype)


def finish_kernel(*refs):
    mine, theirs, out_ref = refs[: len(refs) // 2], refs[len(refs) // 2 : -1], refs[-1]
    core = lax.axis_index("rep")
    for parts, place in ((mine, core), (theirs, 1 - core)):
        total = parts[0][...]
        for part in parts[1:]:
            total = total + part[...].astype(jnp.float32)
        out_ref[place] = total.T


def swap_cores(value):
    return lax.ppermute(value, "rep", [(0, 1), (1, 0)])


def to_far(value, far):
    return lax.ppermute(value, "seq", [(chip, chip ^ far) for chip in range(lax.axis_size("seq"))])


def spread(parts):
    order = sorted(range(1, len(parts)), key=lambda far: -(far & 2) - (far == 3))
    got = {far: to_far(parts[far], far) for far in order}
    return [parts[0]] + [got[far] for far in range(1, len(parts))]


def per_device(
    queries, response_keys, response_values, grad_out, prompt_keys, prompt_values, packing, lengths, tree_mask
):
    slots, seg_length, size = response_keys.shape
    heads = queries.shape[2] // size
    chips = lax.axis_size("seq")
    band = seg_length // chips
    share = prompt_keys.shape[0]
    prompt = share * chips
    rows = slots * seg_length
    core = lax.axis_index("rep")
    xor = band % 16 == 0 and chips == 4
    bf16 = jnp.bfloat16
    sources = (response_keys, response_values, queries, grad_out)

    wanted = lax.dynamic_index_in_dim(packing.reshape(chips, 2, slots), core, 1, keepdims=False)
    if xor:
        tiles = [(0, 0), (1, 0)] + [(source, one) for source in (2, 3) for one in range(heads)]
        counts = [2, 2 * heads]
        high = slots * band
        length = len(tiles) * high
        packed = pl.pallas_call(
            functools.partial(pack_kernel, band, tiles),
            out_shape=[jax.ShapeDtypeStruct((one, size), bf16) for one in [length + share] * 3 + [length] * (chips - 3)],
            in_specs=[HBM] * 6,
            out_specs=[VMEM] * chips,
            scratch_shapes=[pltpu.VMEM(source.shape, bf16) for source in sources] + [pltpu.SemaphoreType.DMA((7,))],
            compiler_params=FULL,
            name="pack",
        )(*sources, prompt_keys, prompt_values)
        mine = spread(packed)
        theirs = [swap_cores(piece) for piece in mine]
        picked = pl.pallas_call(
            functools.partial(pick_kernel, band, chips, counts),
            out_shape=[
                jax.ShapeDtypeStruct((count * high + (2 * share if (number, far) == (0, 1) else 0), size), bf16)
                for number, count in enumerate(counts)
                for far in range(chips)
            ],
            in_specs=[SMEM] + [VMEM] * (2 * chips),
            out_specs=[VMEM] * (chips * len(counts)),
            scratch_shapes=[pltpu.VMEM((2 * chips, len(tiles) * high, size), bf16)],
            compiler_params=SMALL,
            name="pick",
        )(wanted, *mine, *theirs)
        head_rows = spread(picked[chips:])
        pair_rows = spread(picked[:chips])
        prompt_own, prompt_other = mine[:3], theirs[:3]
    else:
        piece = jnp.concatenate(sources, axis=2)
        tiles = piece.shape[2] // size
        piece = piece.reshape(slots, chips, band, tiles, size).transpose(1, 0, 3, 2, 4)
        mine = lax.all_to_all(piece, "seq", split_axis=0, concat_axis=0)
        theirs = swap_cores(mine)
        both = jnp.stack([jnp.where(core == 0, mine, theirs), jnp.where(core == 0, theirs, mine)], axis=1)
        both = both.reshape(chips * 2 * slots, tiles, band, size)
        picked = jnp.take(both, wanted.reshape(-1), axis=0).reshape(chips, slots, tiles, band, size)
        moved = lax.all_to_all(picked, "seq", split_axis=0, concat_axis=0)
        moved = moved.transpose(2, 0, 1, 3, 4).reshape(tiles * rows, size)
        pair_rows, head_rows = [moved[: 2 * rows]], [moved[2 * rows :]]
        prompt_mine = jnp.where(core == 0, prompt_keys, prompt_values)
        prompt_own = [lax.all_gather(prompt_mine, "seq", axis=0, tiled=True)]
        prompt_other = [swap_cores(prompt_own[0])]

    row_count = len(pair_rows)
    high = rows // row_count
    every = prompt + rows
    f32 = jnp.float32
    wide = (slots, seg_length, heads * size) if xor else (heads, rows, size)
    narrow = (slots, seg_length, size) if xor else (1, rows, size)
    parts = [(0, 1), (2, 3)] if xor else [(0,)]
    carried = []
    for bands in parts:
        first, last = bands is parts[0], bands is parts[-1]
        operands = [head_rows[one] for one in bands]
        operands += [*pair_rows, *prompt_own, *prompt_other] if first else carried
        pair_shapes = [jax.ShapeDtypeStruct((every, size), bf16)] * 2
        if last:
            out_shape = [jax.ShapeDtypeStruct(shape, bf16) for shape in (wide, wide, narrow, narrow)]
            out_shape += [jax.ShapeDtypeStruct((row_count, size, prompt // row_count), dtype) for dtype in (f32, bf16)]
        else:
            out_shape = [jax.ShapeDtypeStruct((heads, high * len(bands), size), bf16)] * 2 + pair_shapes
            out_shape += [jax.ShapeDtypeStruct((size, every), f32)] * 2
        count = heads * high * len(bands) * every
        results = pl.pallas_call(
            functools.partial(attend_kernel, band, heads, rows, bands, first, last, xor, row_count),
            out_shape=out_shape,
            in_specs=[SMEM, SMEM] + [VMEM] * len(operands),
            out_specs=[VMEM] * len(out_shape),
            scratch_shapes=[pltpu.VMEM((every, size), bf16)] * 2 if first and last else [],
            compiler_params=LARGE,
            cost_estimate=pl.CostEstimate(
                flops=24 * count * size, bytes_accessed=1 << 20, transcendentals=count
            ),
            name="attend",
        )(lengths, tree_mask, *operands)
        if not last:
            att_part, gq_part, keys, values, key_part, value_part = results
            carried = [keys, values, att_part, gq_part, key_part, value_part]
    attended, grad_queries, grad_keys, grad_values, keep, send = results
    if not xor:

        def restore(value):
            value = value.reshape(-1, chips, slots, band, size).transpose(2, 1, 3, 0, 4)
            return value.reshape(slots, seg_length, -1)

        attended, grad_queries, grad_keys, grad_values = (
            restore(value) for value in (attended, grad_queries, grad_keys, grad_values)
        )

    received = swap_cores(send)
    if xor:
        block = (size, share)
        total = pl.pallas_call(
            combine_kernel,
            out_shape=[jax.ShapeDtypeStruct(block, bf16 if far else jnp.float32) for far in range(chips)],
            in_specs=[VMEM] * 2,
            out_specs=[VMEM] * chips,
            compiler_params=SMALL,
            name="combine",
        )(keep, received)
        arrived = spread(total)
        swapped = [swap_cores(part) for part in arrived]
        prompt_grads = pl.pallas_call(
            finish_kernel,
            out_shape=jax.ShapeDtypeStruct((2, share, size), jnp.float32),
            in_specs=[VMEM] * (2 * chips),
            out_specs=VMEM,
            compiler_params=SMALL,
            name="finish",
        )(*arrived, *swapped)
    else:
        total = (keep + received.astype(jnp.float32)).reshape(size, chips, share).transpose(1, 0, 2).astype(bf16)
        arrived = lax.all_to_all(total, "seq", split_axis=0, concat_axis=0)
        own = jnp.sum(arrived.astype(jnp.float32), axis=0).T
        other = swap_cores(own)
        prompt_grads = jnp.stack([jnp.where(core == 0, own, other), jnp.where(core == 0, other, own)])
    return attended, grad_queries, grad_keys, grad_values, prompt_grads


def solution(mesh):
    segments = P(("groups", "seq", "rep"), None, "head")
    in_specs = (
        segments,
        segments,
        segments,
        segments,
        P(("groups", "seq"), "head"),
        P(("groups", "seq"), "head"),
        P("groups"),
        P(("groups", "seq", "rep")),
        P(("groups", "seq", "rep"), None),
    )
    out_specs = (segments, segments, segments, segments, P(None, ("groups", "seq"), "head"))
    return jax.shard_map(per_device, mesh=mesh, in_specs=in_specs, out_specs=out_specs, check_vma=False)
```

```python
import functools

import jax
import jax.numpy as jnp
from jax import lax
from jax.experimental import pallas as pl
from jax.experimental.pallas import tpu as pltpu
from jax.sharding import PartitionSpec as P

NT = (((1,), (1,)), ((), ()))
NN = (((1,), (0,)), ((), ()))
LOG2E = 1.4426950408889634
GROUPS = (5,)
VMEM = pl.BlockSpec(memory_space=pltpu.VMEM)
HBM = pl.BlockSpec(memory_space=pltpu.HBM)
SMEM = pl.BlockSpec(memory_space=pltpu.SMEM)
SMALL = pltpu.CompilerParams(vmem_limit_bytes=8 * 1024 * 1024)
FULL = pltpu.CompilerParams(vmem_limit_bytes=56 * 1024 * 1024)
LARGE = pltpu.CompilerParams(vmem_limit_bytes=36 * 1024 * 1024)


def dot(left, right, dims):
    return lax.dot_general(left, right, dims, preferred_element_type=jnp.float32)


def pack_kernel(band, tiles, k_hbm, v_hbm, q_hbm, g_hbm, pk_hbm, pv_hbm, *refs):
    chips = len(refs) - 5
    outs, held, sems = refs[:chips], refs[chips:-1], refs[-1]
    me = lax.axis_index("seq")
    core = lax.axis_index("rep")
    share, size = pk_hbm.shape
    rows = len(tiles) * 2 * band
    targets = [out.at[pl.ds(rows, share), :] for out in outs[:3]]
    copies = [
        pltpu.make_async_copy(source, target, sems.at[number])
        for number, (source, target) in enumerate(zip((k_hbm, v_hbm, q_hbm, g_hbm), held))
    ]
    for copy in copies:
        copy.start()

    def prompt_copies(source):
        return [pltpu.make_async_copy(source, target, sems.at[4 + far]) for far, target in enumerate(targets)]

    @pl.when(core == 0)
    def _():
        for copy in prompt_copies(pk_hbm):
            copy.start()

    @pl.when(core != 0)
    def _():
        for copy in prompt_copies(pv_hbm):
            copy.start()

    for copy in copies:
        copy.wait()
    for far, out in enumerate(outs):
        start = pl.multiple_of((me ^ far) * band, 16)
        row = 0
        for source, tile in tiles:
            for slot in range(2):
                out[row : row + band, :] = held[source][slot, pl.ds(start, band), tile * size : (tile + 1) * size]
                row += band
    for copy in prompt_copies(pk_hbm):
        copy.wait()


def pick_kernel(band, chips, counts, wanted_ref, *refs):
    pieces, outs, held = refs[: 2 * chips], list(refs[2 * chips : -1]), refs[-1]
    me = lax.axis_index("seq")
    core = lax.axis_index("rep")
    for number, piece in enumerate(pieces):
        held[number] = piece[: held.shape[1], :]
    near = outs.pop()
    start = sum(counts) * 2 * band
    for piece in (pieces[2], pieces[chips + 2]):
        passed = piece[held.shape[1] :, :]
        near[start : start + passed.shape[0], :] = passed
        start += passed.shape[0]
    for far in range(chips):
        targets = [(near, 0), (near, counts[0])] if far == 1 else [(outs.pop(0), 0), (outs.pop(0), 0)]
        for slot in range(2):
            chosen = wanted_ref[me ^ far, slot]
            device = chosen // 2
            number = ((device // 2) ^ me) + chips * ((device % 2) ^ core)
            tile = 0
            for (out, base), count in zip(targets, counts):
                for one in range(count):
                    start = pl.multiple_of(tile * 2 * band + (chosen % 2) * band, 16)
                    row = (base + one) * 2 * band + slot * band
                    out[row : row + band, :] = held[number, pl.ds(start, band), :]
                    tile += 1


def attend_kernel(band, heads, total_rows, bands, first, last, xor, row_count, length_ref, tree_ref, *refs):
    refs = list(refs)

    def take(count):
        taken = refs[:count]
        del refs[:count]
        return taken

    head_rows = take(len(bands))
    if first:
        pair_rows = take(row_count)
        own_parts, other_parts = take(3 if xor else 1), take(3 if xor else 1)
    else:
        keys, values, att_before, gq_before, key_before, value_before = take(6)
    att_ref, gq_ref = take(2)
    if first:
        keys, values = (refs.pop(-2), refs.pop(-1)) if last else take(2)
    core = lax.axis_index("rep")
    me = lax.axis_index("seq") if xor else 0
    size = keys.shape[1]
    prompt = keys.shape[0] - total_rows
    share = prompt // row_count
    high = total_rows // row_count
    rows = high * len(bands)
    scale = size ** (-0.5)

    def fill(keys_of, values_of):
        for target, pieces in ((keys, keys_of), (values, values_of)):
            for number, (piece, start) in enumerate(pieces):
                target[number * share : (number + 1) * share, :] = piece[start : start + share, :]

    if first:
        own_parts, other_parts = (
            [(piece, piece.shape[0] - share) for piece in parts] for parts in (own_parts, other_parts)
        )
        if xor:
            own_parts.append((pair_rows[1], (2 + 2 * heads) * high))
            other_parts.append((pair_rows[1], (2 + 2 * heads) * high + share))

        @pl.when(core == 0)
        def _():
            fill(own_parts, other_parts)

        @pl.when(core != 0)
        def _():
            fill(other_parts, own_parts)

        for number, pair in enumerate(pair_rows):
            start = prompt + number * high
            keys[start : start + high, :] = pair[:high, :]
            values[start : start + high, :] = pair[high : 2 * high, :]

    def place(shape, axis, start):
        index = lax.broadcasted_iota(jnp.int32, shape, axis) + start
        slot = (index % (2 * band)) // band
        return slot, ((index // (2 * band)) ^ me) * band + index % band

    length_a, length_b = length_ref[0], length_ref[1]
    row_slot, row_at = place((rows, total_rows), 0, bands[0] * high)
    col_slot, col_at = place((rows, total_rows), 1, 0)
    tree = jnp.where(
        row_slot == 0,
        jnp.where(col_slot == 0, tree_ref[0, 0], tree_ref[0, 1]),
        jnp.where(col_slot == 0, tree_ref[1, 0], tree_ref[1, 1]),
    )
    visible = (
        (tree == 1)
        & (col_at < jnp.where(col_slot == 0, length_a, length_b))
        & ((row_slot != col_slot) | (col_at <= row_at))
    )
    slot, at = place((rows, size), 0, bands[0] * high)
    live = (at < jnp.where(slot == 0, length_a, length_b)).astype(jnp.float32)
    live_bf = live.astype(jnp.bfloat16)
    all_keys = keys[...]
    all_values = values[...]

    def put(ref, value, head, placed):
        if not xor:
            ref[head] = value
            return
        for number, which in enumerate(placed):
            for one in range(2):
                start = number * high + one * band
                at = pl.multiple_of((which ^ me) * band, 16)
                ref[one, pl.ds(at, band), head * size : (head + 1) * size] = value[start : start + band, :]

    def rows_of(index):
        parts = []
        for which, ref in zip(bands, head_rows):
            at = (index + 2 if xor and which == 1 else index) * high
            parts.append(ref[at : at + high, :])
        return parts[0] if len(parts) == 1 else jnp.concatenate(parts, axis=0)

    key_total, value_total = (None, None) if first else (key_before[...], value_before[...])
    start = 0
    for count in GROUPS if sum(GROUPS) == heads else (heads,):
        query = jnp.concatenate([rows_of(start + head) for head in range(count)], axis=0)
        grad = jnp.concatenate([rows_of(heads + start + head) * live_bf for head in range(count)], axis=0)
        scores = dot(query, all_keys, NT)
        prompt_scores = scores[:, :prompt]
        tree_scores = jnp.concatenate(
            [jnp.where(visible, scores[head * rows : (head + 1) * rows, prompt:], -1e30) for head in range(count)],
            axis=0,
        )
        top = jnp.maximum(
            jnp.max(prompt_scores, axis=1, keepdims=True), jnp.max(tree_scores, axis=1, keepdims=True)
        )
        scores = jnp.concatenate([prompt_scores, tree_scores], axis=1)
        powers = jnp.exp2((scores - top) * (scale * LOG2E))
        probs = powers * (1.0 / jnp.sum(powers, axis=1, keepdims=True))
        probs_b = probs.astype(jnp.bfloat16)
        attended = dot(probs_b, all_values, NN)
        attended = jnp.concatenate(
            [(attended[head * rows : (head + 1) * rows] * live).astype(jnp.bfloat16) for head in range(count)], axis=0
        )
        delta = jnp.sum(grad.astype(jnp.float32) * attended.astype(jnp.float32), axis=1, keepdims=True)
        dscore = (probs * (dot(grad, all_values, NT) - delta)).astype(jnp.bfloat16)
        grad_query = (dot(dscore, all_keys, NN) * scale).astype(jnp.bfloat16)
        key_part = dot(query.T, dscore, NN)
        value_part = dot(grad.T, probs_b, NN)
        key_total = key_part if key_total is None else key_total + key_part
        value_total = value_part if value_total is None else value_total + value_part
        for head in range(count):
            for ref, result in ((att_ref, attended), (gq_ref, grad_query)):
                result = result[head * rows : (head + 1) * rows, :]
                if last:
                    put(ref, result, start + head, bands)
                else:
                    ref[start + head] = result
        start += count
    if not last:
        refs[0][...] = key_total
        refs[1][...] = value_total
        return
    if not first:
        for head in range(heads):
            for ref, before in ((att_ref, att_before), (gq_ref, gq_before)):
                put(ref, before[head], head, range(bands[0]))
    gk_ref, gv_ref, keep_ref, send_ref = refs
    for ref, result in ((gk_ref, key_total[:, prompt:] * scale), (gv_ref, value_total[:, prompt:])):
        put(ref, result.T.astype(jnp.bfloat16), 0, range(row_count))

    def fill_sums(key_ref, value_ref):
        for number in range(row_count):
            part = slice(number * share, (number + 1) * share)
            key_ref[number] = (key_total[:, part] * scale).astype(key_ref.dtype)
            value_ref[number] = value_total[:, part].astype(value_ref.dtype)

    @pl.when(core == 0)
    def _():
        fill_sums(keep_ref, send_ref)

    @pl.when(core != 0)
    def _():
        fill_sums(send_ref, keep_ref)


def combine_kernel(keep_ref, received_ref, *outs):
    for number, out in enumerate(outs):
        out[...] = (keep_ref[number] + received_ref[number].astype(jnp.float32)).astype(out.dtype)


def add_kernel(part_ref, passed_ref, out_ref):
    out_ref[...] = (part_ref[...] + passed_ref[...].astype(jnp.float32)).astype(out_ref.dtype)


def finish_kernel(*refs):
    mine, theirs, out_ref = refs[: len(refs) // 2], refs[len(refs) // 2 : -1], refs[-1]
    core = lax.axis_index("rep")
    for parts, place in ((mine, core), (theirs, 1 - core)):
        total = parts[0][...]
        for part in parts[1:]:
            total = total + part[...].astype(jnp.float32)
        out_ref[place] = total.T


def swap_cores(value):
    return lax.ppermute(value, "rep", [(0, 1), (1, 0)])


def to_far(value, far):
    return lax.ppermute(value, "seq", [(chip, chip ^ far) for chip in range(lax.axis_size("seq"))])


def spread(parts):
    order = sorted(range(1, len(parts)), key=lambda far: -(far & 2) - (far == 3))
    got = {far: to_far(parts[far], far) for far in order}
    return [parts[0]] + [got[far] for far in range(1, len(parts))]


def per_device(
    queries, response_keys, response_values, grad_out, prompt_keys, prompt_values, packing, lengths, tree_mask
):
    slots, seg_length, size = response_keys.shape
    heads = queries.shape[2] // size
    chips = lax.axis_size("seq")
    band = seg_length // chips
    share = prompt_keys.shape[0]
    prompt = share * chips
    rows = slots * seg_length
    core = lax.axis_index("rep")
    xor = band % 16 == 0 and chips == 4
    bf16 = jnp.bfloat16
    sources = (response_keys, response_values, queries, grad_out)

    wanted = lax.dynamic_index_in_dim(packing.reshape(chips, 2, slots), core, 1, keepdims=False)
    if xor:
        tiles = [(0, 0), (1, 0)] + [(source, one) for source in (2, 3) for one in range(heads)]
        counts = [2, 2 * heads]
        high = slots * band
        length = len(tiles) * high
        packed = pl.pallas_call(
            functools.partial(pack_kernel, band, tiles),
            out_shape=[jax.ShapeDtypeStruct((one, size), bf16) for one in [length + share] * 3 + [length] * (chips - 3)],
            in_specs=[HBM] * 6,
            out_specs=[VMEM] * chips,
            scratch_shapes=[pltpu.VMEM(source.shape, bf16) for source in sources] + [pltpu.SemaphoreType.DMA((7,))],
            compiler_params=FULL,
            name="pack",
        )(*sources, prompt_keys, prompt_values)
        mine = spread(packed)
        theirs = [swap_cores(piece) for piece in mine]
        row_counts = [count * high for count in counts] * (chips - 1) + [length + 2 * share]
        picked = pl.pallas_call(
            functools.partial(pick_kernel, band, chips, counts),
            out_shape=[jax.ShapeDtypeStruct((one, size), bf16) for one in row_counts],
            in_specs=[SMEM] + [VMEM] * (2 * chips),
            out_specs=[VMEM] * len(row_counts),
            scratch_shapes=[pltpu.VMEM((2 * chips, len(tiles) * high, size), bf16)],
            compiler_params=SMALL,
            name="pick",
        )(wanted, mine[0][:length], *mine[1:], *theirs)
        near = to_far(picked[6], 1)
        pair_rows = [picked[0], near, to_far(picked[2], 2), to_far(picked[4], 3)]
        head_rows = [picked[1], near, to_far(picked[3], 2), to_far(picked[5], 3)]
        prompt_own, prompt_other = mine[:3], theirs[:3]
    else:
        piece = jnp.concatenate(sources, axis=2)
        tiles = piece.shape[2] // size
        piece = piece.reshape(slots, chips, band, tiles, size).transpose(1, 0, 3, 2, 4)
        mine = lax.all_to_all(piece, "seq", split_axis=0, concat_axis=0)
        theirs = swap_cores(mine)
        both = jnp.stack([jnp.where(core == 0, mine, theirs), jnp.where(core == 0, theirs, mine)], axis=1)
        both = both.reshape(chips * 2 * slots, tiles, band, size)
        picked = jnp.take(both, wanted.reshape(-1), axis=0).reshape(chips, slots, tiles, band, size)
        moved = lax.all_to_all(picked, "seq", split_axis=0, concat_axis=0)
        moved = moved.transpose(2, 0, 1, 3, 4).reshape(tiles * rows, size)
        pair_rows, head_rows = [moved[: 2 * rows]], [moved[2 * rows :]]
        prompt_mine = jnp.where(core == 0, prompt_keys, prompt_values)
        prompt_own = [lax.all_gather(prompt_mine, "seq", axis=0, tiled=True)]
        prompt_other = [swap_cores(prompt_own[0])]

    row_count = len(pair_rows)
    high = rows // row_count
    every = prompt + rows
    f32 = jnp.float32
    wide = (slots, seg_length, heads * size) if xor else (heads, rows, size)
    narrow = (slots, seg_length, size) if xor else (1, rows, size)
    parts = [(0, 1), (2, 3)] if xor else [(0,)]
    carried = []
    for bands in parts:
        first, last = bands is parts[0], bands is parts[-1]
        operands = [head_rows[one] for one in bands]
        operands += [*pair_rows, *prompt_own, *prompt_other] if first else carried
        pair_shapes = [jax.ShapeDtypeStruct((every, size), bf16)] * 2
        if last:
            out_shape = [jax.ShapeDtypeStruct(shape, bf16) for shape in (wide, wide, narrow, narrow)]
            out_shape += [jax.ShapeDtypeStruct((row_count, size, prompt // row_count), dtype) for dtype in (f32, bf16)]
        else:
            out_shape = [jax.ShapeDtypeStruct((heads, high * len(bands), size), bf16)] * 2 + pair_shapes
            out_shape += [jax.ShapeDtypeStruct((size, every), f32)] * 2
        count = heads * high * len(bands) * every
        results = pl.pallas_call(
            functools.partial(attend_kernel, band, heads, rows, bands, first, last, xor, row_count),
            out_shape=out_shape,
            in_specs=[SMEM, SMEM] + [VMEM] * len(operands),
            out_specs=[VMEM] * len(out_shape),
            scratch_shapes=[pltpu.VMEM((every, size), bf16)] * 2 if first and last else [],
            compiler_params=LARGE,
            cost_estimate=pl.CostEstimate(
                flops=24 * count * size, bytes_accessed=1 << 20, transcendentals=count
            ),
            name="attend",
        )(lengths, tree_mask, *operands)
        if not last:
            att_part, gq_part, keys, values, key_part, value_part = results
            carried = [keys, values, att_part, gq_part, key_part, value_part]
    attended, grad_queries, grad_keys, grad_values, keep, send = results
    if not xor:

        def restore(value):
            value = value.reshape(-1, chips, slots, band, size).transpose(2, 1, 3, 0, 4)
            return value.reshape(slots, seg_length, -1)

        attended, grad_queries, grad_keys, grad_values = (
            restore(value) for value in (attended, grad_queries, grad_keys, grad_values)
        )

    received = swap_cores(send)
    if xor:
        block = (size, share)
        total = pl.pallas_call(
            combine_kernel,
            out_shape=[jax.ShapeDtypeStruct(block, dtype) for dtype in (f32, bf16, f32, bf16)],
            in_specs=[VMEM] * 2,
            out_specs=[VMEM] * chips,
            compiler_params=SMALL,
            name="combine",
        )(keep, received)
        passed = to_far(total[3], 1)
        across = pl.pallas_call(
            add_kernel,
            out_shape=jax.ShapeDtypeStruct(block, bf16),
            in_specs=[VMEM] * 2,
            out_specs=VMEM,
            compiler_params=SMALL,
            name="add",
        )(total[2], passed)
        arrived = [total[0], to_far(total[1], 1), to_far(across, 2)]
        swapped = [swap_cores(part) for part in arrived]
        prompt_grads = pl.pallas_call(
            finish_kernel,
            out_shape=jax.ShapeDtypeStruct((2, share, size), jnp.float32),
            in_specs=[VMEM] * 6,
            out_specs=VMEM,
            compiler_params=SMALL,
            name="finish",
        )(*arrived, *swapped)
    else:
        total = (keep + received.astype(jnp.float32)).reshape(size, chips, share).transpose(1, 0, 2).astype(bf16)
        arrived = lax.all_to_all(total, "seq", split_axis=0, concat_axis=0)
        own = jnp.sum(arrived.astype(jnp.float32), axis=0).T
        other = swap_cores(own)
        prompt_grads = jnp.stack([jnp.where(core == 0, own, other), jnp.where(core == 0, other, own)])
    return attended, grad_queries, grad_keys, grad_values, prompt_grads


def solution(mesh):
    segments = P(("groups", "seq", "rep"), None, "head")
    in_specs = (
        segments,
        segments,
        segments,
        segments,
        P(("groups", "seq"), "head"),
        P(("groups", "seq"), "head"),
        P("groups"),
        P(("groups", "seq", "rep")),
        P(("groups", "seq", "rep"), None),
    )
    out_specs = (segments, segments, segments, segments, P(None, ("groups", "seq"), "head"))
    return jax.shard_map(per_device, mesh=mesh, in_specs=in_specs, out_specs=out_specs, check_vma=False)
```

```python
import functools

import jax
import jax.numpy as jnp
from jax import lax
from jax.experimental import pallas as pl
from jax.experimental.pallas import tpu as pltpu
from jax.sharding import PartitionSpec as P

NT = (((1,), (1,)), ((), ()))
NN = (((1,), (0,)), ((), ()))
LOG2E = 1.4426950408889634
GROUPS = (5,)
VMEM = pl.BlockSpec(memory_space=pltpu.VMEM)
HBM = pl.BlockSpec(memory_space=pltpu.HBM)
SMEM = pl.BlockSpec(memory_space=pltpu.SMEM)
SMALL = pltpu.CompilerParams(vmem_limit_bytes=8 * 1024 * 1024)
FULL = pltpu.CompilerParams(vmem_limit_bytes=56 * 1024 * 1024)
LARGE = pltpu.CompilerParams(vmem_limit_bytes=36 * 1024 * 1024)


def dot(left, right, dims):
    return lax.dot_general(left, right, dims, preferred_element_type=jnp.float32)


def pack_kernel(band, tiles, k_hbm, v_hbm, q_hbm, g_hbm, pk_hbm, pv_hbm, *refs):
    chips = len(refs) - 5
    outs, held, sems = refs[:chips], refs[chips:-1], refs[-1]
    me = lax.axis_index("seq")
    core = lax.axis_index("rep")
    share, size = pk_hbm.shape
    rows = len(tiles) * 2 * band
    targets = [out.at[pl.ds(rows, share), :] for out in outs[:3]]
    copies = [
        pltpu.make_async_copy(source, target, sems.at[number])
        for number, (source, target) in enumerate(zip((k_hbm, v_hbm, q_hbm, g_hbm), held))
    ]
    for copy in copies:
        copy.start()

    def prompt_copies(source):
        return [pltpu.make_async_copy(source, target, sems.at[4 + far]) for far, target in enumerate(targets)]

    @pl.when(core == 0)
    def _():
        for copy in prompt_copies(pk_hbm):
            copy.start()

    @pl.when(core != 0)
    def _():
        for copy in prompt_copies(pv_hbm):
            copy.start()

    for copy in copies:
        copy.wait()
    for far, out in enumerate(outs):
        start = pl.multiple_of((me ^ far) * band, 16)
        row = 0
        for source, tile in tiles:
            for slot in range(2):
                out[row : row + band, :] = held[source][slot, pl.ds(start, band), tile * size : (tile + 1) * size]
                row += band
    for copy in prompt_copies(pk_hbm):
        copy.wait()


def pick_kernel(band, chips, counts, wanted_ref, *refs):
    pieces, outs, held = refs[: 2 * chips], list(refs[2 * chips : -1]), refs[-1]
    me = lax.axis_index("seq")
    core = lax.axis_index("rep")
    for number, piece in enumerate(pieces):
        held[number] = piece[: held.shape[1], :]
    near = outs.pop()
    start = sum(counts) * 2 * band
    for piece in (pieces[2], pieces[chips + 2]):
        passed = piece[held.shape[1] :, :]
        near[start : start + passed.shape[0], :] = passed
        start += passed.shape[0]
    for far in range(chips):
        targets = [(near, 0), (near, counts[0])] if far == 1 else [(outs.pop(0), 0), (outs.pop(0), 0)]
        for slot in range(2):
            chosen = wanted_ref[me ^ far, slot]
            device = chosen // 2
            number = ((device // 2) ^ me) + chips * ((device % 2) ^ core)
            tile = 0
            for (out, base), count in zip(targets, counts):
                for one in range(count):
                    start = pl.multiple_of(tile * 2 * band + (chosen % 2) * band, 16)
                    row = (base + one) * 2 * band + slot * band
                    out[row : row + band, :] = held[number, pl.ds(start, band), :]
                    tile += 1


def attend_kernel(band, heads, total_rows, bands, first, last, xor, row_count, length_ref, tree_ref, *refs):
    refs = list(refs)

    def take(count):
        taken = refs[:count]
        del refs[:count]
        return taken

    head_rows = take(len(bands))
    if first:
        pair_rows = take(row_count)
        own_parts, other_parts = take(3 if xor else 1), take(3 if xor else 1)
    else:
        keys, values, key_before, value_before = take(4)
    att_ref, gq_ref = take(2)
    if first:
        keys, values = (refs.pop(-2), refs.pop(-1)) if last else take(2)
    core = lax.axis_index("rep")
    me = lax.axis_index("seq") if xor else 0
    size = keys.shape[1]
    prompt = keys.shape[0] - total_rows
    share = prompt // row_count
    high = total_rows // row_count
    rows = high * len(bands)
    scale = size ** (-0.5)

    def fill(keys_of, values_of):
        for target, pieces in ((keys, keys_of), (values, values_of)):
            for number, (piece, start) in enumerate(pieces):
                target[number * share : (number + 1) * share, :] = piece[start : start + share, :]

    if first:
        own_parts, other_parts = (
            [(piece, piece.shape[0] - share) for piece in parts] for parts in (own_parts, other_parts)
        )
        if xor:
            own_parts.append((pair_rows[1], (2 + 2 * heads) * high))
            other_parts.append((pair_rows[1], (2 + 2 * heads) * high + share))

        @pl.when(core == 0)
        def _():
            fill(own_parts, other_parts)

        @pl.when(core != 0)
        def _():
            fill(other_parts, own_parts)

        for number, pair in enumerate(pair_rows):
            start = prompt + number * high
            keys[start : start + high, :] = pair[:high, :]
            values[start : start + high, :] = pair[high : 2 * high, :]

    def place(shape, axis, start):
        index = lax.broadcasted_iota(jnp.int32, shape, axis) + start
        slot = (index % (2 * band)) // band
        return slot, ((index // (2 * band)) ^ me) * band + index % band

    length_a, length_b = length_ref[0], length_ref[1]
    row_slot, row_at = place((rows, total_rows), 0, bands[0] * high)
    col_slot, col_at = place((rows, total_rows), 1, 0)
    tree = jnp.where(
        row_slot == 0,
        jnp.where(col_slot == 0, tree_ref[0, 0], tree_ref[0, 1]),
        jnp.where(col_slot == 0, tree_ref[1, 0], tree_ref[1, 1]),
    )
    visible = (
        (tree == 1)
        & (col_at < jnp.where(col_slot == 0, length_a, length_b))
        & ((row_slot != col_slot) | (col_at <= row_at))
    )
    slot, at = place((rows, size), 0, bands[0] * high)
    live = (at < jnp.where(slot == 0, length_a, length_b)).astype(jnp.float32)
    live_bf = live.astype(jnp.bfloat16)
    all_keys = keys[...]
    all_values = values[...]

    def rows_of(index):
        parts = []
        for which, ref in zip(bands, head_rows):
            at = (index + 2 if xor and which == 1 else index) * high
            parts.append(ref[at : at + high, :])
        return parts[0] if len(parts) == 1 else jnp.concatenate(parts, axis=0)

    key_total, value_total = (None, None) if first else (key_before[...], value_before[...])
    start = 0
    for count in GROUPS if sum(GROUPS) == heads else (heads,):
        query = jnp.concatenate([rows_of(start + head) for head in range(count)], axis=0)
        grad = jnp.concatenate([rows_of(heads + start + head) * live_bf for head in range(count)], axis=0)
        scores = dot(query, all_keys, NT)
        prompt_scores = scores[:, :prompt]
        tree_scores = jnp.concatenate(
            [jnp.where(visible, scores[head * rows : (head + 1) * rows, prompt:], -1e30) for head in range(count)],
            axis=0,
        )
        top = jnp.maximum(
            jnp.max(prompt_scores, axis=1, keepdims=True), jnp.max(tree_scores, axis=1, keepdims=True)
        )
        scores = jnp.concatenate([prompt_scores, tree_scores], axis=1)
        powers = jnp.exp2((scores - top) * (scale * LOG2E))
        probs = powers * (1.0 / jnp.sum(powers, axis=1, keepdims=True))
        probs_b = probs.astype(jnp.bfloat16)
        attended = dot(probs_b, all_values, NN)
        attended = jnp.concatenate(
            [(attended[head * rows : (head + 1) * rows] * live).astype(jnp.bfloat16) for head in range(count)], axis=0
        )
        delta = jnp.sum(grad.astype(jnp.float32) * attended.astype(jnp.float32), axis=1, keepdims=True)
        dscore = (probs * (dot(grad, all_values, NT) - delta)).astype(jnp.bfloat16)
        grad_query = (dot(dscore, all_keys, NN) * scale).astype(jnp.bfloat16)
        key_part = dot(query.T, dscore, NN)
        value_part = dot(grad.T, probs_b, NN)
        key_total = key_part if key_total is None else key_total + key_part
        value_total = value_part if value_total is None else value_total + value_part
        for head in range(count):
            for ref, result in ((att_ref, attended), (gq_ref, grad_query)):
                ref[start + head] = result[head * rows : (head + 1) * rows, :]
        start += count
    if not last:
        refs[0][...] = key_total
        refs[1][...] = value_total
        return
    gk_ref, gv_ref, keep_ref, send_ref = refs
    gk_ref[...] = key_total[:, prompt:] * scale
    gv_ref[...] = value_total[:, prompt:]

    def fill_sums(key_ref, value_ref):
        for number in range(row_count):
            part = slice(number * share, (number + 1) * share)
            key_ref[number] = (key_total[:, part] * scale).astype(key_ref.dtype)
            value_ref[number] = value_total[:, part].astype(value_ref.dtype)

    @pl.when(core == 0)
    def _():
        fill_sums(keep_ref, send_ref)

    @pl.when(core != 0)
    def _():
        fill_sums(send_ref, keep_ref)


def place_kernel(band, high, *refs):
    *parts, gk_part, gv_part, att_ref, gq_ref, gk_ref, gv_ref = refs
    me = lax.axis_index("seq")
    size = gk_part.shape[0]

    def put(ref, value, column, which):
        for one in range(2):
            at = pl.multiple_of((which ^ me) * band, 16)
            ref[one, pl.ds(at, band), column * size : (column + 1) * size] = value[one * band : (one + 1) * band, :]

    for ref, pieces in ((att_ref, parts[0::2]), (gq_ref, parts[1::2])):
        for head in range(pieces[0].shape[0]):
            which = 0
            for piece in pieces:
                for start in range(0, piece.shape[1], high):
                    put(ref, piece[head, start : start + high, :], head, which)
                    which += 1
    for ref, part in ((gk_ref, gk_part), (gv_ref, gv_part)):
        rows = part[...].T.astype(jnp.bfloat16)
        for which in range(rows.shape[0] // high):
            put(ref, rows[which * high : (which + 1) * high, :], 0, which)


def combine_kernel(keep_ref, received_ref, *outs):
    for number, out in enumerate(outs):
        out[...] = (keep_ref[number] + received_ref[number].astype(jnp.float32)).astype(out.dtype)


def add_kernel(part_ref, passed_ref, out_ref):
    out_ref[...] = (part_ref[...] + passed_ref[...].astype(jnp.float32)).astype(out_ref.dtype)


def finish_kernel(*refs):
    mine, theirs, out_ref = refs[: len(refs) // 2], refs[len(refs) // 2 : -1], refs[-1]
    core = lax.axis_index("rep")
    for parts, place in ((mine, core), (theirs, 1 - core)):
        total = parts[0][...]
        for part in parts[1:]:
            total = total + part[...].astype(jnp.float32)
        out_ref[place] = total.T


def swap_cores(value):
    return lax.ppermute(value, "rep", [(0, 1), (1, 0)])


def to_far(value, far):
    return lax.ppermute(value, "seq", [(chip, chip ^ far) for chip in range(lax.axis_size("seq"))])


def spread(parts):
    order = sorted(range(1, len(parts)), key=lambda far: -(far & 2) - (far == 3))
    got = {far: to_far(parts[far], far) for far in order}
    return [parts[0]] + [got[far] for far in range(1, len(parts))]


def per_device(
    queries, response_keys, response_values, grad_out, prompt_keys, prompt_values, packing, lengths, tree_mask
):
    slots, seg_length, size = response_keys.shape
    heads = queries.shape[2] // size
    chips = lax.axis_size("seq")
    band = seg_length // chips
    share = prompt_keys.shape[0]
    prompt = share * chips
    rows = slots * seg_length
    core = lax.axis_index("rep")
    xor = band % 16 == 0 and chips == 4
    bf16 = jnp.bfloat16
    sources = (response_keys, response_values, queries, grad_out)

    wanted = lax.dynamic_index_in_dim(packing.reshape(chips, 2, slots), core, 1, keepdims=False)
    if xor:
        tiles = [(0, 0), (1, 0)] + [(source, one) for source in (2, 3) for one in range(heads)]
        counts = [2, 2 * heads]
        high = slots * band
        length = len(tiles) * high
        packed = pl.pallas_call(
            functools.partial(pack_kernel, band, tiles),
            out_shape=[jax.ShapeDtypeStruct((one, size), bf16) for one in [length + share] * 3 + [length] * (chips - 3)],
            in_specs=[HBM] * 6,
            out_specs=[VMEM] * chips,
            scratch_shapes=[pltpu.VMEM(source.shape, bf16) for source in sources] + [pltpu.SemaphoreType.DMA((7,))],
            compiler_params=FULL,
            name="pack",
        )(*sources, prompt_keys, prompt_values)
        mine = spread(packed)
        own_rows, wanted, mine[1] = lax.optimization_barrier((mine[0][:length], wanted, mine[1]))
        theirs = [swap_cores(piece) for piece in mine]
        row_counts = [count * high for count in counts] * (chips - 1) + [length + 2 * share]
        picked = pl.pallas_call(
            functools.partial(pick_kernel, band, chips, counts),
            out_shape=[jax.ShapeDtypeStruct((one, size), bf16) for one in row_counts],
            in_specs=[SMEM] + [VMEM] * (2 * chips),
            out_specs=[VMEM] * len(row_counts),
            scratch_shapes=[pltpu.VMEM((2 * chips, len(tiles) * high, size), bf16)],
            compiler_params=SMALL,
            name="pick",
        )(wanted, own_rows, *mine[1:], *theirs)
        near = to_far(picked[6], 1)
        pair_rows = [picked[0], near, to_far(picked[2], 2), to_far(picked[4], 3)]
        head_rows = [picked[1], near, to_far(picked[3], 2), to_far(picked[5], 3)]
        prompt_own, prompt_other = mine[:3], theirs[:3]
    else:
        piece = jnp.concatenate(sources, axis=2)
        tiles = piece.shape[2] // size
        piece = piece.reshape(slots, chips, band, tiles, size).transpose(1, 0, 3, 2, 4)
        mine = lax.all_to_all(piece, "seq", split_axis=0, concat_axis=0)
        theirs = swap_cores(mine)
        both = jnp.stack([jnp.where(core == 0, mine, theirs), jnp.where(core == 0, theirs, mine)], axis=1)
        both = both.reshape(chips * 2 * slots, tiles, band, size)
        picked = jnp.take(both, wanted.reshape(-1), axis=0).reshape(chips, slots, tiles, band, size)
        moved = lax.all_to_all(picked, "seq", split_axis=0, concat_axis=0)
        moved = moved.transpose(2, 0, 1, 3, 4).reshape(tiles * rows, size)
        pair_rows, head_rows = [moved[: 2 * rows]], [moved[2 * rows :]]
        prompt_mine = jnp.where(core == 0, prompt_keys, prompt_values)
        prompt_own = [lax.all_gather(prompt_mine, "seq", axis=0, tiled=True)]
        prompt_other = [swap_cores(prompt_own[0])]

    row_count = len(pair_rows)
    high = rows // row_count
    every = prompt + rows
    f32 = jnp.float32
    wide, narrow = (slots, seg_length, heads * size), (slots, seg_length, size)
    parts = [(0, 1), (2, 3)] if xor else [(0,)]
    carried, placed = [], []
    for bands in parts:
        first, last = bands is parts[0], bands is parts[-1]
        operands = [head_rows[one] for one in bands]
        operands += [*pair_rows, *prompt_own, *prompt_other] if first else carried
        pair_shapes = [jax.ShapeDtypeStruct((every, size), bf16)] * 2
        out_shape = [jax.ShapeDtypeStruct((heads, high * len(bands), size), bf16)] * 2
        if last:
            out_shape += [jax.ShapeDtypeStruct((size, rows), f32)] * 2
            out_shape += [jax.ShapeDtypeStruct((row_count, size, prompt // row_count), dtype) for dtype in (f32, bf16)]
        else:
            out_shape += pair_shapes + [jax.ShapeDtypeStruct((size, every), f32)] * 2
        count = heads * high * len(bands) * every
        results = pl.pallas_call(
            functools.partial(attend_kernel, band, heads, rows, bands, first, last, xor, row_count),
            out_shape=out_shape,
            in_specs=[SMEM, SMEM] + [VMEM] * len(operands),
            out_specs=[VMEM] * len(out_shape),
            scratch_shapes=[pltpu.VMEM((every, size), bf16)] * 2 if first and last else [],
            compiler_params=LARGE,
            cost_estimate=pl.CostEstimate(
                flops=24 * count * size, bytes_accessed=1 << 20, transcendentals=count
            ),
            name="attend",
        )(lengths, tree_mask, *operands)
        placed += results[:2]
        carried = results[2:]
    placed += carried[:2]
    keep, send = carried[2:]
    if xor:
        outputs = pl.pallas_call(
            functools.partial(place_kernel, band, high),
            out_shape=[jax.ShapeDtypeStruct(shape, bf16) for shape in (wide, wide, narrow, narrow)],
            in_specs=[VMEM] * len(placed),
            out_specs=[VMEM] * 4,
            compiler_params=SMALL,
            name="place",
        )(*placed)
    else:

        def restore(value):
            value = value.reshape(-1, chips, slots, band, size).transpose(2, 1, 3, 0, 4)
            return value.reshape(slots, seg_length, -1)

        outputs = [restore(value) for value in placed[:2]]
        outputs += [restore(value.T.astype(bf16)[None]) for value in placed[2:]]

    received = swap_cores(send)
    if xor:
        block = (size, share)
        total = pl.pallas_call(
            combine_kernel,
            out_shape=[jax.ShapeDtypeStruct(block, dtype) for dtype in (f32, bf16, f32, bf16)],
            in_specs=[VMEM] * 2,
            out_specs=[VMEM] * chips,
            compiler_params=SMALL,
            name="combine",
        )(keep, received)
        passed, *outputs = lax.optimization_barrier((to_far(total[3], 1), *outputs))
        across = pl.pallas_call(
            add_kernel,
            out_shape=jax.ShapeDtypeStruct(block, bf16),
            in_specs=[VMEM] * 2,
            out_specs=VMEM,
            compiler_params=SMALL,
            name="add",
        )(total[2], passed)
        arrived = [total[0], to_far(total[1], 1), to_far(across, 2)]
        swapped = [swap_cores(part) for part in arrived]
        prompt_grads = pl.pallas_call(
            finish_kernel,
            out_shape=jax.ShapeDtypeStruct((2, share, size), jnp.float32),
            in_specs=[VMEM] * 6,
            out_specs=VMEM,
            compiler_params=SMALL,
            name="finish",
        )(*arrived, *swapped)
    else:
        total = (keep + received.astype(jnp.float32)).reshape(size, chips, share).transpose(1, 0, 2).astype(bf16)
        arrived = lax.all_to_all(total, "seq", split_axis=0, concat_axis=0)
        own = jnp.sum(arrived.astype(jnp.float32), axis=0).T
        other = swap_cores(own)
        prompt_grads = jnp.stack([jnp.where(core == 0, own, other), jnp.where(core == 0, other, own)])
    return *outputs, prompt_grads


def solution(mesh):
    segments = P(("groups", "seq", "rep"), None, "head")
    in_specs = (
        segments,
        segments,
        segments,
        segments,
        P(("groups", "seq"), "head"),
        P(("groups", "seq"), "head"),
        P("groups"),
        P(("groups", "seq", "rep")),
        P(("groups", "seq", "rep"), None),
    )
    out_specs = (segments, segments, segments, segments, P(None, ("groups", "seq"), "head"))
    return jax.shard_map(per_device, mesh=mesh, in_specs=in_specs, out_specs=out_specs, check_vma=False)
```

```python
import functools

import jax
import jax.numpy as jnp
from jax import lax
from jax.experimental import pallas as pl
from jax.experimental.pallas import tpu as pltpu
from jax.sharding import PartitionSpec as P

NT = (((1,), (1,)), ((), ()))
NN = (((1,), (0,)), ((), ()))
LOG2E = 1.4426950408889634
GROUPS = (5,)
VMEM = pl.BlockSpec(memory_space=pltpu.VMEM)
HBM = pl.BlockSpec(memory_space=pltpu.HBM)
SMEM = pl.BlockSpec(memory_space=pltpu.SMEM)
SMALL = pltpu.CompilerParams(vmem_limit_bytes=8 * 1024 * 1024)
FULL = pltpu.CompilerParams(vmem_limit_bytes=56 * 1024 * 1024)
LARGE = pltpu.CompilerParams(vmem_limit_bytes=36 * 1024 * 1024)


def dot(left, right, dims):
    return lax.dot_general(left, right, dims, preferred_element_type=jnp.float32)


def pack_kernel(band, tiles, fars, k_hbm, v_hbm, q_hbm, g_hbm, pk_hbm, pv_hbm, *refs):
    outs, held, sems = refs[: len(fars)], refs[len(fars) : -1], refs[-1]
    me = lax.axis_index("seq")
    core = lax.axis_index("rep")
    share, size = pk_hbm.shape
    rows = len(tiles) * 2 * band
    targets = [out.at[pl.ds(rows, share), :] for far, out in zip(fars, outs) if far < 3]
    copies = [
        pltpu.make_async_copy(source, target, sems.at[number])
        for number, (source, target) in enumerate(zip((k_hbm, v_hbm, q_hbm, g_hbm), held))
    ]
    for copy in copies:
        copy.start()

    def prompt_copies(source):
        return [pltpu.make_async_copy(source, target, sems.at[4 + one]) for one, target in enumerate(targets)]

    @pl.when(core == 0)
    def _():
        for copy in prompt_copies(pk_hbm):
            copy.start()

    @pl.when(core != 0)
    def _():
        for copy in prompt_copies(pv_hbm):
            copy.start()

    for copy in copies:
        copy.wait()
    for far, out in zip(fars, outs):
        start = pl.multiple_of((me ^ far) * band, 16)
        row = 0
        for source, tile in tiles:
            for slot in range(2):
                out[row : row + band, :] = held[source][slot, pl.ds(start, band), tile * size : (tile + 1) * size]
                row += band
    for copy in prompt_copies(pk_hbm):
        copy.wait()


def pick_kernel(band, chips, counts, wanted_ref, *refs):
    pieces, outs, held = refs[: 2 * chips], list(refs[2 * chips : -1]), refs[-1]
    me = lax.axis_index("seq")
    core = lax.axis_index("rep")
    for number, piece in enumerate(pieces):
        held[number] = piece[: held.shape[1], :]
    near = outs.pop()
    start = sum(counts) * 2 * band
    for piece in (pieces[2], pieces[chips + 2]):
        passed = piece[held.shape[1] :, :]
        near[start : start + passed.shape[0], :] = passed
        start += passed.shape[0]
    for far in range(chips):
        targets = [(near, 0), (near, counts[0])] if far == 1 else [(outs.pop(0), 0), (outs.pop(0), 0)]
        for slot in range(2):
            chosen = wanted_ref[me ^ far, slot]
            device = chosen // 2
            number = ((device // 2) ^ me) + chips * ((device % 2) ^ core)
            tile = 0
            for (out, base), count in zip(targets, counts):
                for one in range(count):
                    start = pl.multiple_of(tile * 2 * band + (chosen % 2) * band, 16)
                    row = (base + one) * 2 * band + slot * band
                    out[row : row + band, :] = held[number, pl.ds(start, band), :]
                    tile += 1


def attend_kernel(band, heads, total_rows, bands, first, last, xor, row_count, length_ref, tree_ref, *refs):
    refs = list(refs)

    def take(count):
        taken = refs[:count]
        del refs[:count]
        return taken

    head_rows = take(len(bands))
    if first:
        pair_rows = take(row_count)
        own_parts, other_parts = take(3 if xor else 1), take(3 if xor else 1)
    else:
        keys, values, key_before, value_before = take(4)
    att_ref, gq_ref = take(2)
    if first:
        keys, values = (refs.pop(-2), refs.pop(-1)) if last else take(2)
    core = lax.axis_index("rep")
    me = lax.axis_index("seq") if xor else 0
    size = keys.shape[1]
    prompt = keys.shape[0] - total_rows
    share = prompt // row_count
    high = total_rows // row_count
    rows = high * len(bands)
    scale = size ** (-0.5)

    def fill(keys_of, values_of):
        for target, pieces in ((keys, keys_of), (values, values_of)):
            for number, (piece, start) in enumerate(pieces):
                target[number * share : (number + 1) * share, :] = piece[start : start + share, :]

    if first:
        own_parts, other_parts = (
            [(piece, piece.shape[0] - share) for piece in parts] for parts in (own_parts, other_parts)
        )
        if xor:
            own_parts.append((pair_rows[1], (2 + 2 * heads) * high))
            other_parts.append((pair_rows[1], (2 + 2 * heads) * high + share))

        @pl.when(core == 0)
        def _():
            fill(own_parts, other_parts)

        @pl.when(core != 0)
        def _():
            fill(other_parts, own_parts)

        for number, pair in enumerate(pair_rows):
            start = prompt + number * high
            keys[start : start + high, :] = pair[:high, :]
            values[start : start + high, :] = pair[high : 2 * high, :]

    def place(shape, axis, start):
        index = lax.broadcasted_iota(jnp.int32, shape, axis) + start
        slot = (index % (2 * band)) // band
        return slot, ((index // (2 * band)) ^ me) * band + index % band

    length_a, length_b = length_ref[0], length_ref[1]
    row_slot, row_at = place((rows, total_rows), 0, bands[0] * high)
    col_slot, col_at = place((rows, total_rows), 1, 0)
    tree = jnp.where(
        row_slot == 0,
        jnp.where(col_slot == 0, tree_ref[0, 0], tree_ref[0, 1]),
        jnp.where(col_slot == 0, tree_ref[1, 0], tree_ref[1, 1]),
    )
    visible = (
        (tree == 1)
        & (col_at < jnp.where(col_slot == 0, length_a, length_b))
        & ((row_slot != col_slot) | (col_at <= row_at))
    )
    slot, at = place((rows, size), 0, bands[0] * high)
    live = (at < jnp.where(slot == 0, length_a, length_b)).astype(jnp.float32)
    live_bf = live.astype(jnp.bfloat16)
    all_keys = keys[...]
    all_values = values[...]

    def rows_of(index):
        parts = []
        for which, ref in zip(bands, head_rows):
            at = (index + 2 if xor and which == 1 else index) * high
            parts.append(ref[at : at + high, :])
        return parts[0] if len(parts) == 1 else jnp.concatenate(parts, axis=0)

    key_total, value_total = (None, None) if first else (key_before[...], value_before[...])
    start = 0
    for count in GROUPS if sum(GROUPS) == heads else (heads,):
        query = jnp.concatenate([rows_of(start + head) for head in range(count)], axis=0)
        grad = jnp.concatenate([rows_of(heads + start + head) * live_bf for head in range(count)], axis=0)
        scores = dot(query, all_keys, NT)
        prompt_scores = scores[:, :prompt]
        tree_scores = jnp.concatenate(
            [jnp.where(visible, scores[head * rows : (head + 1) * rows, prompt:], -1e30) for head in range(count)],
            axis=0,
        )
        top = jnp.maximum(
            jnp.max(prompt_scores, axis=1, keepdims=True), jnp.max(tree_scores, axis=1, keepdims=True)
        )
        scores = jnp.concatenate([prompt_scores, tree_scores], axis=1)
        powers = jnp.exp2((scores - top) * (scale * LOG2E))
        probs = powers * (1.0 / jnp.sum(powers, axis=1, keepdims=True))
        probs_b = probs.astype(jnp.bfloat16)
        attended = dot(probs_b, all_values, NN)
        attended = jnp.concatenate(
            [(attended[head * rows : (head + 1) * rows] * live).astype(jnp.bfloat16) for head in range(count)], axis=0
        )
        delta = jnp.sum(grad.astype(jnp.float32) * attended.astype(jnp.float32), axis=1, keepdims=True)
        dscore = (probs * (dot(grad, all_values, NT) - delta)).astype(jnp.bfloat16)
        grad_query = (dot(dscore, all_keys, NN) * scale).astype(jnp.bfloat16)
        key_part = dot(query.T, dscore, NN)
        value_part = dot(grad.T, probs_b, NN)
        key_total = key_part if key_total is None else key_total + key_part
        value_total = value_part if value_total is None else value_total + value_part
        for head in range(count):
            for ref, result in ((att_ref, attended), (gq_ref, grad_query)):
                ref[start + head] = result[head * rows : (head + 1) * rows, :]
        start += count
    if not last:
        refs[0][...] = key_total
        refs[1][...] = value_total
        return
    gk_ref, gv_ref, keep_ref, send_ref = refs
    gk_ref[...] = key_total[:, prompt:] * scale
    gv_ref[...] = value_total[:, prompt:]

    def fill_sums(key_ref, value_ref):
        for number in range(row_count):
            part = slice(number * share, (number + 1) * share)
            key_ref[number] = (key_total[:, part] * scale).astype(key_ref.dtype)
            value_ref[number] = value_total[:, part].astype(value_ref.dtype)

    @pl.when(core == 0)
    def _():
        fill_sums(keep_ref, send_ref)

    @pl.when(core != 0)
    def _():
        fill_sums(send_ref, keep_ref)


def place_kernel(band, high, *refs):
    *parts, gk_part, gv_part, att_ref, gq_ref, gk_ref, gv_ref = refs
    me = lax.axis_index("seq")
    size = gk_part.shape[0]

    def put(ref, value, column, which):
        for one in range(2):
            at = pl.multiple_of((which ^ me) * band, 16)
            ref[one, pl.ds(at, band), column * size : (column + 1) * size] = value[one * band : (one + 1) * band, :]

    for ref, pieces in ((att_ref, parts[0::2]), (gq_ref, parts[1::2])):
        for head in range(pieces[0].shape[0]):
            which = 0
            for piece in pieces:
                for start in range(0, piece.shape[1], high):
                    put(ref, piece[head, start : start + high, :], head, which)
                    which += 1
    for ref, part in ((gk_ref, gk_part), (gv_ref, gv_part)):
        rows = part[...].T.astype(jnp.bfloat16)
        for which in range(rows.shape[0] // high):
            put(ref, rows[which * high : (which + 1) * high, :], 0, which)


def combine_kernel(keep_ref, received_ref, *outs):
    for number, out in enumerate(outs):
        out[...] = (keep_ref[number] + received_ref[number].astype(jnp.float32)).astype(out.dtype)


def finish_kernel(*refs):
    mine, theirs, out_ref = refs[: len(refs) // 2], refs[len(refs) // 2 : -1], refs[-1]
    core = lax.axis_index("rep")
    for parts, place in ((mine, core), (theirs, 1 - core)):
        total = parts[0][...]
        for part in parts[1:]:
            total = total + part[...].astype(jnp.float32)
        out_ref[place] = total.T


def swap_cores(value):
    return lax.ppermute(value, "rep", [(0, 1), (1, 0)])


def to_far(value, far):
    return lax.ppermute(value, "seq", [(chip, chip ^ far) for chip in range(lax.axis_size("seq"))])


def spread(parts):
    order = sorted(range(1, len(parts)), key=lambda far: -(far & 2) - (far == 3))
    got = {far: to_far(parts[far], far) for far in order}
    return [parts[0]] + [got[far] for far in range(1, len(parts))]


def per_device(
    queries, response_keys, response_values, grad_out, prompt_keys, prompt_values, packing, lengths, tree_mask
):
    slots, seg_length, size = response_keys.shape
    heads = queries.shape[2] // size
    chips = lax.axis_size("seq")
    band = seg_length // chips
    share = prompt_keys.shape[0]
    prompt = share * chips
    rows = slots * seg_length
    core = lax.axis_index("rep")
    xor = band % 16 == 0 and chips == 4
    bf16 = jnp.bfloat16
    sources = (response_keys, response_values, queries, grad_out)

    wanted = lax.dynamic_index_in_dim(packing.reshape(chips, 2, slots), core, 1, keepdims=False)
    if xor:
        tiles = [(0, 0), (1, 0)] + [(source, one) for source in (2, 3) for one in range(heads)]
        counts = [2, 2 * heads]
        high = slots * band
        length = len(tiles) * high
        packed = {}
        for fars in ((1, 2, 3), (0,)):
            messages = pl.pallas_call(
                functools.partial(pack_kernel, band, tiles, fars),
                out_shape=[jax.ShapeDtypeStruct((length + share * (far < 3), size), bf16) for far in fars],
                in_specs=[HBM] * 6,
                out_specs=[VMEM] * len(fars),
                scratch_shapes=[pltpu.VMEM(source.shape, bf16) for source in sources] + [pltpu.SemaphoreType.DMA((6,))],
                compiler_params=FULL,
                name="pack",
            )(*sources, prompt_keys, prompt_values)
            packed.update(zip(fars, messages))
        packed = [packed[far] for far in range(chips)]
        mine = spread(packed)
        own_rows, wanted, mine[1] = lax.optimization_barrier((mine[0][:length], wanted, mine[1]))
        theirs = [swap_cores(piece) for piece in mine]
        row_counts = [count * high for count in counts] * (chips - 1) + [length + 2 * share]
        picked = pl.pallas_call(
            functools.partial(pick_kernel, band, chips, counts),
            out_shape=[jax.ShapeDtypeStruct((one, size), bf16) for one in row_counts],
            in_specs=[SMEM] + [VMEM] * (2 * chips),
            out_specs=[VMEM] * len(row_counts),
            scratch_shapes=[pltpu.VMEM((2 * chips, len(tiles) * high, size), bf16)],
            compiler_params=SMALL,
            name="pick",
        )(wanted, own_rows, *mine[1:], *theirs)
        near = to_far(picked[6], 1)
        pair_rows = [picked[0], near, to_far(picked[2], 2), to_far(picked[4], 3)]
        head_rows = [picked[1], near, to_far(picked[3], 2), to_far(picked[5], 3)]
        prompt_own, prompt_other = mine[:3], theirs[:3]
    else:
        piece = jnp.concatenate(sources, axis=2)
        tiles = piece.shape[2] // size
        piece = piece.reshape(slots, chips, band, tiles, size).transpose(1, 0, 3, 2, 4)
        mine = lax.all_to_all(piece, "seq", split_axis=0, concat_axis=0)
        theirs = swap_cores(mine)
        both = jnp.stack([jnp.where(core == 0, mine, theirs), jnp.where(core == 0, theirs, mine)], axis=1)
        both = both.reshape(chips * 2 * slots, tiles, band, size)
        picked = jnp.take(both, wanted.reshape(-1), axis=0).reshape(chips, slots, tiles, band, size)
        moved = lax.all_to_all(picked, "seq", split_axis=0, concat_axis=0)
        moved = moved.transpose(2, 0, 1, 3, 4).reshape(tiles * rows, size)
        pair_rows, head_rows = [moved[: 2 * rows]], [moved[2 * rows :]]
        prompt_mine = jnp.where(core == 0, prompt_keys, prompt_values)
        prompt_own = [lax.all_gather(prompt_mine, "seq", axis=0, tiled=True)]
        prompt_other = [swap_cores(prompt_own[0])]

    row_count = len(pair_rows)
    high = rows // row_count
    every = prompt + rows
    f32 = jnp.float32
    wide, narrow = (slots, seg_length, heads * size), (slots, seg_length, size)
    parts = [(0, 1), (2, 3)] if xor else [(0,)]
    carried, placed = [], []
    for bands in parts:
        first, last = bands is parts[0], bands is parts[-1]
        operands = [head_rows[one] for one in bands]
        operands += [*pair_rows, *prompt_own, *prompt_other] if first else carried
        pair_shapes = [jax.ShapeDtypeStruct((every, size), bf16)] * 2
        out_shape = [jax.ShapeDtypeStruct((heads, high * len(bands), size), bf16)] * 2
        if last:
            out_shape += [jax.ShapeDtypeStruct((size, rows), f32)] * 2
            out_shape += [jax.ShapeDtypeStruct((row_count, size, prompt // row_count), dtype) for dtype in (f32, bf16)]
        else:
            out_shape += pair_shapes + [jax.ShapeDtypeStruct((size, every), f32)] * 2
        count = heads * high * len(bands) * every
        results = pl.pallas_call(
            functools.partial(attend_kernel, band, heads, rows, bands, first, last, xor, row_count),
            out_shape=out_shape,
            in_specs=[SMEM, SMEM] + [VMEM] * len(operands),
            out_specs=[VMEM] * len(out_shape),
            scratch_shapes=[pltpu.VMEM((every, size), bf16)] * 2 if first and last else [],
            compiler_params=LARGE,
            cost_estimate=pl.CostEstimate(
                flops=24 * count * size, bytes_accessed=1 << 20, transcendentals=count
            ),
            name="attend",
        )(lengths, tree_mask, *operands)
        placed += results[:2]
        carried = results[2:]
    placed += carried[:2]
    keep, send = carried[2:]
    if xor:
        outputs = pl.pallas_call(
            functools.partial(place_kernel, band, high),
            out_shape=[jax.ShapeDtypeStruct(shape, bf16) for shape in (wide, wide, narrow, narrow)],
            in_specs=[VMEM] * len(placed),
            out_specs=[VMEM] * 4,
            compiler_params=SMALL,
            name="place",
        )(*placed)
    else:

        def restore(value):
            value = value.reshape(-1, chips, slots, band, size).transpose(2, 1, 3, 0, 4)
            return value.reshape(slots, seg_length, -1)

        outputs = [restore(value) for value in placed[:2]]
        outputs += [restore(value.T.astype(bf16)[None]) for value in placed[2:]]

    received = swap_cores(send)
    if xor:
        block = (size, share)
        total = pl.pallas_call(
            combine_kernel,
            out_shape=[jax.ShapeDtypeStruct(block, dtype) for dtype in (f32, bf16, bf16, bf16)],
            in_specs=[VMEM] * 2,
            out_specs=[VMEM] * chips,
            compiler_params=SMALL,
            name="combine",
        )(keep, received)
        arrived = spread(total)
        arrived[1], *outputs = lax.optimization_barrier((arrived[1], *outputs))
        swapped = [swap_cores(part) for part in arrived]
        prompt_grads = pl.pallas_call(
            finish_kernel,
            out_shape=jax.ShapeDtypeStruct((2, share, size), jnp.float32),
            in_specs=[VMEM] * (2 * chips),
            out_specs=VMEM,
            compiler_params=SMALL,
            name="finish",
        )(*arrived, *swapped)
    else:
        total = (keep + received.astype(jnp.float32)).reshape(size, chips, share).transpose(1, 0, 2).astype(bf16)
        arrived = lax.all_to_all(total, "seq", split_axis=0, concat_axis=0)
        own = jnp.sum(arrived.astype(jnp.float32), axis=0).T
        other = swap_cores(own)
        prompt_grads = jnp.stack([jnp.where(core == 0, own, other), jnp.where(core == 0, other, own)])
    return *outputs, prompt_grads


def solution(mesh):
    segments = P(("groups", "seq", "rep"), None, "head")
    in_specs = (
        segments,
        segments,
        segments,
        segments,
        P(("groups", "seq"), "head"),
        P(("groups", "seq"), "head"),
        P("groups"),
        P(("groups", "seq", "rep")),
        P(("groups", "seq", "rep"), None),
    )
    out_specs = (segments, segments, segments, segments, P(None, ("groups", "seq"), "head"))
    return jax.shard_map(per_device, mesh=mesh, in_specs=in_specs, out_specs=out_specs, check_vma=False)
```

```python
import functools

import jax
import jax.numpy as jnp
from jax import lax
from jax.experimental import pallas as pl
from jax.experimental.pallas import tpu as pltpu
from jax.sharding import PartitionSpec as P

NT = (((1,), (1,)), ((), ()))
NN = (((1,), (0,)), ((), ()))
LOG2E = 1.4426950408889634
GROUPS = (5,)
VMEM = pl.BlockSpec(memory_space=pltpu.VMEM)
HBM = pl.BlockSpec(memory_space=pltpu.HBM)
SMEM = pl.BlockSpec(memory_space=pltpu.SMEM)
SMALL = pltpu.CompilerParams(vmem_limit_bytes=8 * 1024 * 1024)
FULL = pltpu.CompilerParams(vmem_limit_bytes=56 * 1024 * 1024)
LARGE = pltpu.CompilerParams(vmem_limit_bytes=36 * 1024 * 1024)


def dot(left, right, dims):
    return lax.dot_general(left, right, dims, preferred_element_type=jnp.float32)


def pack_kernel(band, tiles, fars, k_hbm, v_hbm, q_hbm, g_hbm, pk_hbm, pv_hbm, *refs):
    outs, held, sems = refs[: len(fars)], refs[len(fars) : -1], refs[-1]
    me = lax.axis_index("seq")
    core = lax.axis_index("rep")
    share, size = pk_hbm.shape
    rows = len(tiles) * 2 * band
    targets = [out.at[pl.ds(rows, share), :] for far, out in zip(fars, outs) if far < 3]
    copies = [
        pltpu.make_async_copy(source, target, sems.at[number])
        for number, (source, target) in enumerate(zip((k_hbm, v_hbm, q_hbm, g_hbm), held))
    ]
    for copy in copies:
        copy.start()

    def prompt_copies(source):
        return [pltpu.make_async_copy(source, target, sems.at[4 + one]) for one, target in enumerate(targets)]

    @pl.when(core == 0)
    def _():
        for copy in prompt_copies(pk_hbm):
            copy.start()

    @pl.when(core != 0)
    def _():
        for copy in prompt_copies(pv_hbm):
            copy.start()

    for copy in copies:
        copy.wait()
    for far, out in zip(fars, outs):
        start = pl.multiple_of((me ^ far) * band, 16)
        row = 0
        for source, tile in tiles:
            for slot in range(2):
                out[row : row + band, :] = held[source][slot, pl.ds(start, band), tile * size : (tile + 1) * size]
                row += band
    for copy in prompt_copies(pk_hbm):
        copy.wait()


def pick_kernel(band, chips, counts, wanted_ref, *refs):
    pieces, outs, held = refs[: 2 * chips], list(refs[2 * chips : -1]), refs[-1]
    me = lax.axis_index("seq")
    core = lax.axis_index("rep")
    for number, piece in enumerate(pieces):
        held[number] = piece[: held.shape[1], :]
    near = outs.pop()
    start = sum(counts) * 2 * band
    for piece in (pieces[2], pieces[chips + 2]):
        passed = piece[held.shape[1] :, :]
        near[start : start + passed.shape[0], :] = passed
        start += passed.shape[0]
    for far in range(chips):
        targets = [(near, 0), (near, counts[0])] if far == 1 else [(outs.pop(0), 0), (outs.pop(0), 0)]
        for slot in range(2):
            chosen = wanted_ref[me ^ far, slot]
            device = chosen // 2
            number = ((device // 2) ^ me) + chips * ((device % 2) ^ core)
            tile = 0
            for (out, base), count in zip(targets, counts):
                for one in range(count):
                    start = pl.multiple_of(tile * 2 * band + (chosen % 2) * band, 16)
                    row = (base + one) * 2 * band + slot * band
                    out[row : row + band, :] = held[number, pl.ds(start, band), :]
                    tile += 1


def attend_kernel(band, heads, total_rows, bands, first, last, xor, row_count, length_ref, tree_ref, *refs):
    refs = list(refs)

    def take(count):
        taken = refs[:count]
        del refs[:count]
        return taken

    head_rows = take(len(bands))
    if first:
        pair_rows = take(row_count)
        own_parts, other_parts = take(3 if xor else 1), take(3 if xor else 1)
    else:
        keys, values, key_before, value_before = take(4)
    att_ref, gq_ref = take(2)
    if first:
        keys, values = (refs.pop(-2), refs.pop(-1)) if last else take(2)
    core = lax.axis_index("rep")
    me = lax.axis_index("seq") if xor else 0
    size = keys.shape[1]
    prompt = keys.shape[0] - total_rows
    share = prompt // row_count
    high = total_rows // row_count
    rows = high * len(bands)
    scale = size ** (-0.5)

    def fill(keys_of, values_of):
        for target, pieces in ((keys, keys_of), (values, values_of)):
            for number, (piece, start) in enumerate(pieces):
                target[number * share : (number + 1) * share, :] = piece[start : start + share, :]

    if first:
        own_parts, other_parts = (
            [(piece, piece.shape[0] - share) for piece in parts] for parts in (own_parts, other_parts)
        )
        if xor:
            own_parts.append((pair_rows[1], (2 + 2 * heads) * high))
            other_parts.append((pair_rows[1], (2 + 2 * heads) * high + share))

        @pl.when(core == 0)
        def _():
            fill(own_parts, other_parts)

        @pl.when(core != 0)
        def _():
            fill(other_parts, own_parts)

        for number, pair in enumerate(pair_rows):
            start = prompt + number * high
            keys[start : start + high, :] = pair[:high, :]
            values[start : start + high, :] = pair[high : 2 * high, :]

    def place(shape, axis, start):
        index = lax.broadcasted_iota(jnp.int32, shape, axis) + start
        slot = (index % (2 * band)) // band
        return slot, ((index // (2 * band)) ^ me) * band + index % band

    length_a, length_b = length_ref[0], length_ref[1]
    row_slot, row_at = place((rows, total_rows), 0, bands[0] * high)
    col_slot, col_at = place((rows, total_rows), 1, 0)
    tree = jnp.where(
        row_slot == 0,
        jnp.where(col_slot == 0, tree_ref[0, 0], tree_ref[0, 1]),
        jnp.where(col_slot == 0, tree_ref[1, 0], tree_ref[1, 1]),
    )
    visible = (
        (tree == 1)
        & (col_at < jnp.where(col_slot == 0, length_a, length_b))
        & ((row_slot != col_slot) | (col_at <= row_at))
    )
    slot, at = place((rows, size), 0, bands[0] * high)
    live = (at < jnp.where(slot == 0, length_a, length_b)).astype(jnp.float32)
    live_bf = live.astype(jnp.bfloat16)
    all_keys = keys[...]
    all_values = values[...]

    def rows_of(index):
        parts = []
        for which, ref in zip(bands, head_rows):
            at = (index + 2 if xor and which == 1 else index) * high
            parts.append(ref[at : at + high, :])
        return parts[0] if len(parts) == 1 else jnp.concatenate(parts, axis=0)

    key_total, value_total = (None, None) if first else (key_before[...], value_before[...])
    start = 0
    for count in GROUPS if sum(GROUPS) == heads else (heads,):
        query = jnp.concatenate([rows_of(start + head) for head in range(count)], axis=0)
        grad = jnp.concatenate([rows_of(heads + start + head) * live_bf for head in range(count)], axis=0)
        scores = dot(query, all_keys, NT)
        prompt_scores = scores[:, :prompt]
        tree_scores = jnp.concatenate(
            [jnp.where(visible, scores[head * rows : (head + 1) * rows, prompt:], -1e30) for head in range(count)],
            axis=0,
        )
        top = jnp.maximum(
            jnp.max(prompt_scores, axis=1, keepdims=True), jnp.max(tree_scores, axis=1, keepdims=True)
        )
        scores = jnp.concatenate([prompt_scores, tree_scores], axis=1)
        powers = jnp.exp2((scores - top) * (scale * LOG2E))
        probs = powers * (1.0 / jnp.sum(powers, axis=1, keepdims=True))
        probs_b = probs.astype(jnp.bfloat16)
        attended = dot(probs_b, all_values, NN)
        attended = jnp.concatenate(
            [(attended[head * rows : (head + 1) * rows] * live).astype(jnp.bfloat16) for head in range(count)], axis=0
        )
        delta = jnp.sum(grad.astype(jnp.float32) * attended.astype(jnp.float32), axis=1, keepdims=True)
        dscore = (probs * (dot(grad, all_values, NT) - delta)).astype(jnp.bfloat16)
        grad_query = (dot(dscore, all_keys, NN) * scale).astype(jnp.bfloat16)
        key_part = dot(query.T, dscore, NN)
        value_part = dot(grad.T, probs_b, NN)
        key_total = key_part if key_total is None else key_total + key_part
        value_total = value_part if value_total is None else value_total + value_part
        for head in range(count):
            for ref, result in ((att_ref, attended), (gq_ref, grad_query)):
                ref[start + head] = result[head * rows : (head + 1) * rows, :]
        start += count
    if not last:
        refs[0][...] = key_total
        refs[1][...] = value_total
        return
    gk_ref, gv_ref, keep_ref, send_ref = refs
    gk_ref[...] = key_total[:, prompt:] * scale
    gv_ref[...] = value_total[:, prompt:]

    def fill_sums(key_ref, value_ref):
        for number in range(row_count):
            part = slice(number * share, (number + 1) * share)
            key_ref[number] = (key_total[:, part] * scale).astype(key_ref.dtype)
            value_ref[number] = value_total[:, part].astype(value_ref.dtype)

    @pl.when(core == 0)
    def _():
        fill_sums(keep_ref, send_ref)

    @pl.when(core != 0)
    def _():
        fill_sums(send_ref, keep_ref)


def place_kernel(band, high, *refs):
    *parts, gk_part, gv_part, att_ref, gq_ref, gk_ref, gv_ref = refs
    me = lax.axis_index("seq")
    size = gk_part.shape[0]

    def put(ref, value, column, which):
        for one in range(2):
            at = pl.multiple_of((which ^ me) * band, 16)
            ref[one, pl.ds(at, band), column * size : (column + 1) * size] = value[one * band : (one + 1) * band, :]

    for ref, pieces in ((att_ref, parts[0::2]), (gq_ref, parts[1::2])):
        for head in range(pieces[0].shape[0]):
            which = 0
            for piece in pieces:
                for start in range(0, piece.shape[1], high):
                    put(ref, piece[head, start : start + high, :], head, which)
                    which += 1
    for ref, part in ((gk_ref, gk_part), (gv_ref, gv_part)):
        rows = part[...].T.astype(jnp.bfloat16)
        for which in range(rows.shape[0] // high):
            put(ref, rows[which * high : (which + 1) * high, :], 0, which)


def combine_kernel(keep_ref, received_ref, *outs):
    for number, out in enumerate(outs):
        out[...] = (keep_ref[number] + received_ref[number].astype(jnp.float32)).astype(out.dtype)


def finish_kernel(other, *refs):
    *parts, out_hbm, held, sem = refs
    core = lax.axis_index("rep")
    if other:
        parts = parts[1:]
    total = parts[0][...]
    for part in parts[1:]:
        total = total + part[...].astype(jnp.float32)
    held[...] = total.T
    copy = pltpu.make_async_copy(held, out_hbm.at[1 - core if other else core], sem)
    copy.start()
    copy.wait()


def swap_cores(value):
    return lax.ppermute(value, "rep", [(0, 1), (1, 0)])


def to_far(value, far):
    return lax.ppermute(value, "seq", [(chip, chip ^ far) for chip in range(lax.axis_size("seq"))])


def spread(parts):
    order = sorted(range(1, len(parts)), key=lambda far: -(far & 2) - (far == 3))
    got = {far: to_far(parts[far], far) for far in order}
    return [parts[0]] + [got[far] for far in range(1, len(parts))]


def per_device(
    queries, response_keys, response_values, grad_out, prompt_keys, prompt_values, packing, lengths, tree_mask
):
    slots, seg_length, size = response_keys.shape
    heads = queries.shape[2] // size
    chips = lax.axis_size("seq")
    band = seg_length // chips
    share = prompt_keys.shape[0]
    prompt = share * chips
    rows = slots * seg_length
    core = lax.axis_index("rep")
    xor = band % 16 == 0 and chips == 4
    bf16 = jnp.bfloat16
    sources = (response_keys, response_values, queries, grad_out)

    wanted = lax.dynamic_index_in_dim(packing.reshape(chips, 2, slots), core, 1, keepdims=False)
    if xor:
        tiles = [(0, 0), (1, 0)] + [(source, one) for source in (2, 3) for one in range(heads)]
        counts = [2, 2 * heads]
        high = slots * band
        length = len(tiles) * high
        packed = {}
        for fars in ((1, 2, 3), (0,)):
            messages = pl.pallas_call(
                functools.partial(pack_kernel, band, tiles, fars),
                out_shape=[jax.ShapeDtypeStruct((length + share * (far < 3), size), bf16) for far in fars],
                in_specs=[HBM] * 6,
                out_specs=[VMEM] * len(fars),
                scratch_shapes=[pltpu.VMEM(source.shape, bf16) for source in sources] + [pltpu.SemaphoreType.DMA((6,))],
                compiler_params=FULL,
                name="pack",
            )(*sources, prompt_keys, prompt_values)
            packed.update(zip(fars, messages))
        packed = [packed[far] for far in range(chips)]
        mine = spread(packed)
        own_rows, wanted, mine[1] = lax.optimization_barrier((mine[0][:length], wanted, mine[1]))
        theirs = [swap_cores(piece) for piece in mine]
        row_counts = [count * high for count in counts] * (chips - 1) + [length + 2 * share]
        picked = pl.pallas_call(
            functools.partial(pick_kernel, band, chips, counts),
            out_shape=[jax.ShapeDtypeStruct((one, size), bf16) for one in row_counts],
            in_specs=[SMEM] + [VMEM] * (2 * chips),
            out_specs=[VMEM] * len(row_counts),
            scratch_shapes=[pltpu.VMEM((2 * chips, len(tiles) * high, size), bf16)],
            compiler_params=SMALL,
            name="pick",
        )(wanted, own_rows, *mine[1:], *theirs)
        near = to_far(picked[6], 1)
        pair_rows = [picked[0], near, to_far(picked[2], 2), to_far(picked[4], 3)]
        head_rows = [picked[1], near, to_far(picked[3], 2), to_far(picked[5], 3)]
        prompt_own, prompt_other = mine[:3], theirs[:3]
    else:
        piece = jnp.concatenate(sources, axis=2)
        tiles = piece.shape[2] // size
        piece = piece.reshape(slots, chips, band, tiles, size).transpose(1, 0, 3, 2, 4)
        mine = lax.all_to_all(piece, "seq", split_axis=0, concat_axis=0)
        theirs = swap_cores(mine)
        both = jnp.stack([jnp.where(core == 0, mine, theirs), jnp.where(core == 0, theirs, mine)], axis=1)
        both = both.reshape(chips * 2 * slots, tiles, band, size)
        picked = jnp.take(both, wanted.reshape(-1), axis=0).reshape(chips, slots, tiles, band, size)
        moved = lax.all_to_all(picked, "seq", split_axis=0, concat_axis=0)
        moved = moved.transpose(2, 0, 1, 3, 4).reshape(tiles * rows, size)
        pair_rows, head_rows = [moved[: 2 * rows]], [moved[2 * rows :]]
        prompt_mine = jnp.where(core == 0, prompt_keys, prompt_values)
        prompt_own = [lax.all_gather(prompt_mine, "seq", axis=0, tiled=True)]
        prompt_other = [swap_cores(prompt_own[0])]

    row_count = len(pair_rows)
    high = rows // row_count
    every = prompt + rows
    f32 = jnp.float32
    wide, narrow = (slots, seg_length, heads * size), (slots, seg_length, size)
    parts = [(0, 1), (2, 3)] if xor else [(0,)]
    carried, placed = [], []
    for bands in parts:
        first, last = bands is parts[0], bands is parts[-1]
        operands = [head_rows[one] for one in bands]
        operands += [*pair_rows, *prompt_own, *prompt_other] if first else carried
        pair_shapes = [jax.ShapeDtypeStruct((every, size), bf16)] * 2
        out_shape = [jax.ShapeDtypeStruct((heads, high * len(bands), size), bf16)] * 2
        if last:
            out_shape += [jax.ShapeDtypeStruct((size, rows), f32)] * 2
            out_shape += [jax.ShapeDtypeStruct((row_count, size, prompt // row_count), dtype) for dtype in (f32, bf16)]
        else:
            out_shape += pair_shapes + [jax.ShapeDtypeStruct((size, every), f32)] * 2
        count = heads * high * len(bands) * every
        results = pl.pallas_call(
            functools.partial(attend_kernel, band, heads, rows, bands, first, last, xor, row_count),
            out_shape=out_shape,
            in_specs=[SMEM, SMEM] + [VMEM] * len(operands),
            out_specs=[VMEM] * len(out_shape),
            scratch_shapes=[pltpu.VMEM((every, size), bf16)] * 2 if first and last else [],
            compiler_params=LARGE,
            cost_estimate=pl.CostEstimate(
                flops=24 * count * size, bytes_accessed=1 << 20, transcendentals=count
            ),
            name="attend",
        )(lengths, tree_mask, *operands)
        placed += results[:2]
        carried = results[2:]
    placed += carried[:2]
    keep, send = carried[2:]
    if xor:
        outputs = pl.pallas_call(
            functools.partial(place_kernel, band, high),
            out_shape=[jax.ShapeDtypeStruct(shape, bf16) for shape in (wide, wide, narrow, narrow)],
            in_specs=[VMEM] * len(placed),
            out_specs=[VMEM] * 4,
            compiler_params=SMALL,
            name="place",
        )(*placed)
    else:

        def restore(value):
            value = value.reshape(-1, chips, slots, band, size).transpose(2, 1, 3, 0, 4)
            return value.reshape(slots, seg_length, -1)

        outputs = [restore(value) for value in placed[:2]]
        outputs += [restore(value.T.astype(bf16)[None]) for value in placed[2:]]

    received = swap_cores(send)
    if xor:
        block = (size, share)
        total = pl.pallas_call(
            combine_kernel,
            out_shape=[jax.ShapeDtypeStruct(block, dtype) for dtype in (f32, bf16, bf16, bf16)],
            in_specs=[VMEM] * 2,
            out_specs=[VMEM] * chips,
            compiler_params=SMALL,
            name="combine",
        )(keep, received)
        arrived = spread(total)
        arrived[1], *outputs = lax.optimization_barrier((arrived[1], *outputs))
        swapped = [swap_cores(part) for part in arrived]
        prompt_grads = ()
        for other, parts in enumerate((arrived, swapped)):
            prompt_grads = pl.pallas_call(
                functools.partial(finish_kernel, other),
                out_shape=jax.ShapeDtypeStruct((2, share, size), jnp.float32),
                in_specs=[HBM] * other + [VMEM] * chips,
                out_specs=HBM,
                scratch_shapes=[pltpu.VMEM((share, size), jnp.float32), pltpu.SemaphoreType.DMA],
                input_output_aliases={0: 0} if other else {},
                compiler_params=SMALL,
                name="finish",
            )(*([prompt_grads] if other else []), *parts)
    else:
        total = (keep + received.astype(jnp.float32)).reshape(size, chips, share).transpose(1, 0, 2).astype(bf16)
        arrived = lax.all_to_all(total, "seq", split_axis=0, concat_axis=0)
        own = jnp.sum(arrived.astype(jnp.float32), axis=0).T
        other = swap_cores(own)
        prompt_grads = jnp.stack([jnp.where(core == 0, own, other), jnp.where(core == 0, other, own)])
    return *outputs, prompt_grads


def solution(mesh):
    segments = P(("groups", "seq", "rep"), None, "head")
    in_specs = (
        segments,
        segments,
        segments,
        segments,
        P(("groups", "seq"), "head"),
        P(("groups", "seq"), "head"),
        P("groups"),
        P(("groups", "seq", "rep")),
        P(("groups", "seq", "rep"), None),
    )
    out_specs = (segments, segments, segments, segments, P(None, ("groups", "seq"), "head"))
    return jax.shard_map(per_device, mesh=mesh, in_specs=in_specs, out_specs=out_specs, check_vma=False)
```

```python
import functools

import jax
import jax.numpy as jnp
from jax import lax
from jax.experimental import pallas as pl
from jax.experimental.pallas import tpu as pltpu
from jax.sharding import PartitionSpec as P

NT = (((1,), (1,)), ((), ()))
NN = (((1,), (0,)), ((), ()))
LOG2E = 1.4426950408889634
GROUPS = (5,)
VMEM = pl.BlockSpec(memory_space=pltpu.VMEM)
HBM = pl.BlockSpec(memory_space=pltpu.HBM)
SMEM = pl.BlockSpec(memory_space=pltpu.SMEM)
SMALL = pltpu.CompilerParams(vmem_limit_bytes=8 * 1024 * 1024)
FULL = pltpu.CompilerParams(vmem_limit_bytes=56 * 1024 * 1024)
LARGE = pltpu.CompilerParams(vmem_limit_bytes=36 * 1024 * 1024)


def dot(left, right, dims):
    return lax.dot_general(left, right, dims, preferred_element_type=jnp.float32)


def pack_kernel(band, tiles, fars, k_hbm, v_hbm, q_hbm, g_hbm, pk_hbm, pv_hbm, *refs):
    outs, held, sems = refs[: len(fars)], refs[len(fars) : -1], refs[-1]
    me = lax.axis_index("seq")
    core = lax.axis_index("rep")
    share, size = pk_hbm.shape
    rows = len(tiles) * 2 * band
    targets = [out.at[pl.ds(rows, share), :] for far, out in zip(fars, outs) if far < 3]
    copies = [
        pltpu.make_async_copy(source, target, sems.at[number])
        for number, (source, target) in enumerate(zip((k_hbm, v_hbm, q_hbm, g_hbm), held))
    ]
    for copy in copies:
        copy.start()

    def prompt_copies(source):
        return [pltpu.make_async_copy(source, target, sems.at[4 + one]) for one, target in enumerate(targets)]

    @pl.when(core == 0)
    def _():
        for copy in prompt_copies(pk_hbm):
            copy.start()

    @pl.when(core != 0)
    def _():
        for copy in prompt_copies(pv_hbm):
            copy.start()

    for copy in copies:
        copy.wait()
    for far, out in zip(fars, outs):
        start = pl.multiple_of((me ^ far) * band, 16)
        row = 0
        for source, tile in tiles:
            for slot in range(2):
                out[row : row + band, :] = held[source][slot, pl.ds(start, band), tile * size : (tile + 1) * size]
                row += band
    for copy in prompt_copies(pk_hbm):
        copy.wait()


def pick_kernel(band, chips, counts, wanted_ref, *refs):
    pieces, outs, held = refs[: 2 * chips], list(refs[2 * chips : -1]), refs[-1]
    me = lax.axis_index("seq")
    core = lax.axis_index("rep")
    for number, piece in enumerate(pieces):
        held[number] = piece[: held.shape[1], :]
    near = outs.pop()
    start = sum(counts) * 2 * band
    for piece in (pieces[2], pieces[chips + 2]):
        passed = piece[held.shape[1] :, :]
        near[start : start + passed.shape[0], :] = passed
        start += passed.shape[0]
    for far in range(chips):
        targets = [(near, 0), (near, counts[0])] if far == 1 else [(outs.pop(0), 0), (outs.pop(0), 0)]
        for slot in range(2):
            chosen = wanted_ref[me ^ far, slot]
            device = chosen // 2
            number = ((device // 2) ^ me) + chips * ((device % 2) ^ core)
            tile = 0
            for (out, base), count in zip(targets, counts):
                for one in range(count):
                    start = pl.multiple_of(tile * 2 * band + (chosen % 2) * band, 16)
                    row = (base + one) * 2 * band + slot * band
                    out[row : row + band, :] = held[number, pl.ds(start, band), :]
                    tile += 1


def attend_kernel(band, heads, total_rows, bands, first, last, xor, row_count, length_ref, tree_ref, *refs):
    refs = list(refs)

    def take(count):
        taken = refs[:count]
        del refs[:count]
        return taken

    head_rows = take(len(bands))
    if first:
        pair_rows = take(row_count)
        own_parts, other_parts = take(3 if xor else 1), take(3 if xor else 1)
    else:
        keys, values, key_before, value_before = take(4)
    att_ref, gq_ref = take(2)
    if first:
        keys, values = (refs.pop(-2), refs.pop(-1)) if last else take(2)
    core = lax.axis_index("rep")
    me = lax.axis_index("seq") if xor else 0
    size = keys.shape[1]
    prompt = keys.shape[0] - total_rows
    share = prompt // row_count
    high = total_rows // row_count
    rows = high * len(bands)
    scale = size ** (-0.5)

    def fill(keys_of, values_of):
        for target, pieces in ((keys, keys_of), (values, values_of)):
            for number, (piece, start) in enumerate(pieces):
                target[number * share : (number + 1) * share, :] = piece[start : start + share, :]

    if first:
        own_parts, other_parts = (
            [(piece, piece.shape[0] - share) for piece in parts] for parts in (own_parts, other_parts)
        )
        if xor:
            own_parts.append((pair_rows[1], (2 + 2 * heads) * high))
            other_parts.append((pair_rows[1], (2 + 2 * heads) * high + share))

        @pl.when(core == 0)
        def _():
            fill(own_parts, other_parts)

        @pl.when(core != 0)
        def _():
            fill(other_parts, own_parts)

        for number, pair in enumerate(pair_rows):
            start = prompt + number * high
            keys[start : start + high, :] = pair[:high, :]
            values[start : start + high, :] = pair[high : 2 * high, :]

    def place(shape, axis, start):
        index = lax.broadcasted_iota(jnp.int32, shape, axis) + start
        slot = (index % (2 * band)) // band
        return slot, ((index // (2 * band)) ^ me) * band + index % band

    length_a, length_b = length_ref[0], length_ref[1]
    row_slot, row_at = place((rows, total_rows), 0, bands[0] * high)
    col_slot, col_at = place((rows, total_rows), 1, 0)
    tree = jnp.where(
        row_slot == 0,
        jnp.where(col_slot == 0, tree_ref[0, 0], tree_ref[0, 1]),
        jnp.where(col_slot == 0, tree_ref[1, 0], tree_ref[1, 1]),
    )
    visible = (
        (tree == 1)
        & (col_at < jnp.where(col_slot == 0, length_a, length_b))
        & ((row_slot != col_slot) | (col_at <= row_at))
    )
    slot, at = place((rows, size), 0, bands[0] * high)
    live = (at < jnp.where(slot == 0, length_a, length_b)).astype(jnp.float32)
    live_bf = live.astype(jnp.bfloat16)
    all_keys = keys[...]
    all_values = values[...]

    def rows_of(index):
        parts = []
        for which, ref in zip(bands, head_rows):
            at = (index + 2 if xor and which == 1 else index) * high
            parts.append(ref[at : at + high, :])
        return parts[0] if len(parts) == 1 else jnp.concatenate(parts, axis=0)

    key_total, value_total = (None, None) if first else (key_before[...], value_before[...])
    start = 0
    for count in GROUPS if sum(GROUPS) == heads else (heads,):
        query = jnp.concatenate([rows_of(start + head) for head in range(count)], axis=0)
        grad = jnp.concatenate([rows_of(heads + start + head) * live_bf for head in range(count)], axis=0)
        scores = dot(query, all_keys, NT)
        prompt_scores = scores[:, :prompt]
        tree_scores = jnp.concatenate(
            [jnp.where(visible, scores[head * rows : (head + 1) * rows, prompt:], -1e30) for head in range(count)],
            axis=0,
        )
        top = jnp.maximum(
            jnp.max(prompt_scores, axis=1, keepdims=True), jnp.max(tree_scores, axis=1, keepdims=True)
        )
        scores = jnp.concatenate([prompt_scores, tree_scores], axis=1)
        powers = jnp.exp2((scores - top) * (scale * LOG2E))
        probs = powers * (1.0 / jnp.sum(powers, axis=1, keepdims=True))
        probs_b = probs.astype(jnp.bfloat16)
        attended = dot(probs_b, all_values, NN)
        attended = jnp.concatenate(
            [(attended[head * rows : (head + 1) * rows] * live).astype(jnp.bfloat16) for head in range(count)], axis=0
        )
        delta = jnp.sum(grad.astype(jnp.float32) * attended.astype(jnp.float32), axis=1, keepdims=True)
        dscore = (probs * (dot(grad, all_values, NT) - delta)).astype(jnp.bfloat16)
        grad_query = (dot(dscore, all_keys, NN) * scale).astype(jnp.bfloat16)
        key_part = dot(query.T, dscore, NN)
        value_part = dot(grad.T, probs_b, NN)
        key_total = key_part if key_total is None else key_total + key_part
        value_total = value_part if value_total is None else value_total + value_part
        for head in range(count):
            for ref, result in ((att_ref, attended), (gq_ref, grad_query)):
                ref[start + head] = result[head * rows : (head + 1) * rows, :]
        start += count
    if not last:
        refs[0][...] = key_total
        refs[1][...] = value_total
        return
    gk_ref, gv_ref, keep_ref, send_ref = refs
    gk_ref[...] = key_total[:, prompt:] * scale
    gv_ref[...] = value_total[:, prompt:]

    def fill_sums(key_ref, value_ref):
        for number in range(row_count):
            part = slice(number * share, (number + 1) * share)
            key_ref[number] = (key_total[:, part] * scale).astype(key_ref.dtype)
            value_ref[number] = value_total[:, part].astype(value_ref.dtype)

    @pl.when(core == 0)
    def _():
        fill_sums(keep_ref, send_ref)

    @pl.when(core != 0)
    def _():
        fill_sums(send_ref, keep_ref)


def place_kernel(band, high, *refs):
    *parts, gk_part, gv_part, att_ref, gq_ref, gk_ref, gv_ref = refs
    me = lax.axis_index("seq")
    size = gk_part.shape[0]

    def put(ref, value, column, which):
        for one in range(2):
            at = pl.multiple_of((which ^ me) * band, 16)
            ref[one, pl.ds(at, band), column * size : (column + 1) * size] = value[one * band : (one + 1) * band, :]

    for ref, pieces in ((att_ref, parts[0::2]), (gq_ref, parts[1::2])):
        for head in range(pieces[0].shape[0]):
            which = 0
            for piece in pieces:
                for start in range(0, piece.shape[1], high):
                    put(ref, piece[head, start : start + high, :], head, which)
                    which += 1
    for ref, part in ((gk_ref, gk_part), (gv_ref, gv_part)):
        rows = part[...].T.astype(jnp.bfloat16)
        for which in range(rows.shape[0] // high):
            put(ref, rows[which * high : (which + 1) * high, :], 0, which)


def combine_kernel(keep_ref, received_ref, *outs):
    for number, out in enumerate(outs):
        out[...] = (keep_ref[number] + received_ref[number].astype(jnp.float32)).astype(out.dtype)


def finish_kernel(other, *refs):
    *parts, out_hbm, held, sem = refs
    core = lax.axis_index("rep")
    if other:
        parts = parts[1:]
    total = parts[0][...]
    for part in parts[1:]:
        total = total + part[...].astype(jnp.float32)
    held[...] = total.T
    copy = pltpu.make_async_copy(held, out_hbm.at[1 - core if other else core], sem)
    copy.start()
    copy.wait()


def swap_cores(value):
    return lax.ppermute(value, "rep", [(0, 1), (1, 0)])


def to_far(value, far):
    return lax.ppermute(value, "seq", [(chip, chip ^ far) for chip in range(lax.axis_size("seq"))])


def spread(parts):
    order = sorted(range(1, len(parts)), key=lambda far: -(far & 2) - (far == 3))
    got = {far: to_far(parts[far], far) for far in order}
    return [parts[0]] + [got[far] for far in range(1, len(parts))]


def per_device(
    queries, response_keys, response_values, grad_out, prompt_keys, prompt_values, packing, lengths, tree_mask
):
    slots, seg_length, size = response_keys.shape
    heads = queries.shape[2] // size
    chips = lax.axis_size("seq")
    band = seg_length // chips
    share = prompt_keys.shape[0]
    prompt = share * chips
    rows = slots * seg_length
    core = lax.axis_index("rep")
    xor = band % 16 == 0 and chips == 4
    bf16 = jnp.bfloat16
    sources = (response_keys, response_values, queries, grad_out)

    wanted = lax.dynamic_index_in_dim(packing.reshape(chips, 2, slots), core, 1, keepdims=False)
    if xor:
        tiles = [(0, 0), (1, 0)] + [(source, one) for source in (2, 3) for one in range(heads)]
        counts = [2, 2 * heads]
        high = slots * band
        length = len(tiles) * high
        packed = {}
        for fars in ((1, 2, 3), (0,)):
            messages = pl.pallas_call(
                functools.partial(pack_kernel, band, tiles, fars),
                out_shape=[jax.ShapeDtypeStruct((length + share * (far < 3), size), bf16) for far in fars],
                in_specs=[HBM] * 6,
                out_specs=[VMEM] * len(fars),
                scratch_shapes=[pltpu.VMEM(source.shape, bf16) for source in sources] + [pltpu.SemaphoreType.DMA((6,))],
                compiler_params=FULL if len(fars) > 1 else SMALL,
                name="pack",
            )(*sources, prompt_keys, prompt_values)
            packed.update(zip(fars, messages))
        packed = [packed[far] for far in range(chips)]
        mine = spread(packed)
        own_rows, wanted, mine[1] = lax.optimization_barrier((mine[0][:length], wanted, mine[1]))
        theirs = [swap_cores(piece) for piece in mine]
        row_counts = [count * high for count in counts] * (chips - 1) + [length + 2 * share]
        picked = pl.pallas_call(
            functools.partial(pick_kernel, band, chips, counts),
            out_shape=[jax.ShapeDtypeStruct((one, size), bf16) for one in row_counts],
            in_specs=[SMEM] + [VMEM] * (2 * chips),
            out_specs=[VMEM] * len(row_counts),
            scratch_shapes=[pltpu.VMEM((2 * chips, len(tiles) * high, size), bf16)],
            compiler_params=SMALL,
            name="pick",
        )(wanted, own_rows, *mine[1:], *theirs)
        near = to_far(picked[6], 1)
        pair_rows = [picked[0], near, to_far(picked[2], 2), to_far(picked[4], 3)]
        head_rows = [picked[1], near, to_far(picked[3], 2), to_far(picked[5], 3)]
        prompt_own, prompt_other = mine[:3], theirs[:3]
    else:
        piece = jnp.concatenate(sources, axis=2)
        tiles = piece.shape[2] // size
        piece = piece.reshape(slots, chips, band, tiles, size).transpose(1, 0, 3, 2, 4)
        mine = lax.all_to_all(piece, "seq", split_axis=0, concat_axis=0)
        theirs = swap_cores(mine)
        both = jnp.stack([jnp.where(core == 0, mine, theirs), jnp.where(core == 0, theirs, mine)], axis=1)
        both = both.reshape(chips * 2 * slots, tiles, band, size)
        picked = jnp.take(both, wanted.reshape(-1), axis=0).reshape(chips, slots, tiles, band, size)
        moved = lax.all_to_all(picked, "seq", split_axis=0, concat_axis=0)
        moved = moved.transpose(2, 0, 1, 3, 4).reshape(tiles * rows, size)
        pair_rows, head_rows = [moved[: 2 * rows]], [moved[2 * rows :]]
        prompt_mine = jnp.where(core == 0, prompt_keys, prompt_values)
        prompt_own = [lax.all_gather(prompt_mine, "seq", axis=0, tiled=True)]
        prompt_other = [swap_cores(prompt_own[0])]

    row_count = len(pair_rows)
    high = rows // row_count
    every = prompt + rows
    f32 = jnp.float32
    wide, narrow = (slots, seg_length, heads * size), (slots, seg_length, size)
    parts = [(0, 1), (2, 3)] if xor else [(0,)]
    carried, placed = [], []
    for bands in parts:
        first, last = bands is parts[0], bands is parts[-1]
        operands = [head_rows[one] for one in bands]
        operands += [*pair_rows, *prompt_own, *prompt_other] if first else carried
        pair_shapes = [jax.ShapeDtypeStruct((every, size), bf16)] * 2
        out_shape = [jax.ShapeDtypeStruct((heads, high * len(bands), size), bf16)] * 2
        if last:
            out_shape += [jax.ShapeDtypeStruct((size, rows), f32)] * 2
            out_shape += [jax.ShapeDtypeStruct((row_count, size, prompt // row_count), dtype) for dtype in (f32, bf16)]
        else:
            out_shape += pair_shapes + [jax.ShapeDtypeStruct((size, every), f32)] * 2
        count = heads * high * len(bands) * every
        results = pl.pallas_call(
            functools.partial(attend_kernel, band, heads, rows, bands, first, last, xor, row_count),
            out_shape=out_shape,
            in_specs=[SMEM, SMEM] + [VMEM] * len(operands),
            out_specs=[VMEM] * len(out_shape),
            scratch_shapes=[pltpu.VMEM((every, size), bf16)] * 2 if first and last else [],
            compiler_params=LARGE,
            cost_estimate=pl.CostEstimate(
                flops=24 * count * size, bytes_accessed=1 << 20, transcendentals=count
            ),
            name="attend",
        )(lengths, tree_mask, *operands)
        placed += results[:2]
        carried = results[2:]
    placed += carried[:2]
    keep, send = carried[2:]
    if xor:
        outputs = pl.pallas_call(
            functools.partial(place_kernel, band, high),
            out_shape=[jax.ShapeDtypeStruct(shape, bf16) for shape in (wide, wide, narrow, narrow)],
            in_specs=[VMEM] * len(placed),
            out_specs=[VMEM] * 4,
            compiler_params=SMALL,
            name="place",
        )(*placed)
    else:

        def restore(value):
            value = value.reshape(-1, chips, slots, band, size).transpose(2, 1, 3, 0, 4)
            return value.reshape(slots, seg_length, -1)

        outputs = [restore(value) for value in placed[:2]]
        outputs += [restore(value.T.astype(bf16)[None]) for value in placed[2:]]

    received = swap_cores(send)
    if xor:
        block = (size, share)
        total = pl.pallas_call(
            combine_kernel,
            out_shape=[jax.ShapeDtypeStruct(block, dtype) for dtype in (f32, bf16, bf16, bf16)],
            in_specs=[VMEM] * 2,
            out_specs=[VMEM] * chips,
            compiler_params=SMALL,
            name="combine",
        )(keep, received)
        arrived = spread(total)
        arrived[1], *outputs = lax.optimization_barrier((arrived[1], *outputs))
        swapped = [swap_cores(part) for part in arrived]
        prompt_grads = ()
        for other, parts in enumerate((arrived, swapped)):
            prompt_grads = pl.pallas_call(
                functools.partial(finish_kernel, other),
                out_shape=jax.ShapeDtypeStruct((2, share, size), jnp.float32),
                in_specs=[HBM] * other + [VMEM] * chips,
                out_specs=HBM,
                scratch_shapes=[pltpu.VMEM((share, size), jnp.float32), pltpu.SemaphoreType.DMA],
                input_output_aliases={0: 0} if other else {},
                compiler_params=SMALL,
                name="finish",
            )(*([prompt_grads] if other else []), *parts)
    else:
        total = (keep + received.astype(jnp.float32)).reshape(size, chips, share).transpose(1, 0, 2).astype(bf16)
        arrived = lax.all_to_all(total, "seq", split_axis=0, concat_axis=0)
        own = jnp.sum(arrived.astype(jnp.float32), axis=0).T
        other = swap_cores(own)
        prompt_grads = jnp.stack([jnp.where(core == 0, own, other), jnp.where(core == 0, other, own)])
    return *outputs, prompt_grads


def solution(mesh):
    segments = P(("groups", "seq", "rep"), None, "head")
    in_specs = (
        segments,
        segments,
        segments,
        segments,
        P(("groups", "seq"), "head"),
        P(("groups", "seq"), "head"),
        P("groups"),
        P(("groups", "seq", "rep")),
        P(("groups", "seq", "rep"), None),
    )
    out_specs = (segments, segments, segments, segments, P(None, ("groups", "seq"), "head"))
    return jax.shard_map(per_device, mesh=mesh, in_specs=in_specs, out_specs=out_specs, check_vma=False)
```
